256 devices in a mesh: dp: 64 (over z_hi, y, x, core), mp: 4 (over z_lo).
Axes of the slice: x: 4, y: 4, z: 8 (z_hi: 2, z_lo: 4; z = z_hi * 4 + z_lo), core: 2. Of those that a mesh axis runs over, the one named last changes fastest.
Arguments:
- acts: bfloat16 [32768, 4096], P('dp'), may hold values from -12 to 12
- out_grads: bfloat16 [32768, 5120], P('dp', 'mp'), may hold values from -12 to 12
- owners: int32 [4, 9], P('mp'), may hold values from 0 to 63, as said below
Outputs:
- update: bfloat16 [4096, 5120], P('dp', 'mp')
- kept_roots: bfloat16 [128, 1024, 256], P('dp', 'mp')
The draws below stay inside these ranges and needn't reach their ends.
Inputs may be any that keep to these rules, and one draw needn't show every extreme that they name: `owners`: in each row, every index of dp owns at most 2 entries, and some index owns exactly 2.
All inputs are finite; a program needn't handle non-finite values.
Results may differ from the reference program's by a relative error of at most 0.0074.
The reference program's roundings to bfloat16 on the way count: a program that leaves them out, or rounds other values in their place, can miss the bound.
Values may be sent and summed in bfloat16 or wider, within the bound.
No kernel may reach another device: no remote copies, remote signals or barrier semaphores. Data moves between devices by JAX's collectives and lax.ppermute only.
A program may use at most 128 MiB of HBM per device.

```python
import math
import jax
import jax.numpy as jnp
from jax import lax

D = 4096
FFW = 5120
BS = 256
ITERS = 12
MOST = 2
TOKENS = 32768
DBLK = 4
FBLK = 5
NBLK = 9
N_DP = 64
N_MP = 4


def couple(base, col_scale, coupling):
    mixed = (base + coupling * jnp.roll(base, 1, axis=1)) / math.sqrt(1.0 + coupling * coupling)
    return jnp.clip(mixed * col_scale[None, :], -12.0, 12.0)


def draw_acts(key, part):
    key = jax.random.fold_in(key, 1)
    first, second = jax.random.split(key, 2)
    base = jax.random.normal(first, (TOKENS, D))
    col_scale = jnp.exp(jax.random.uniform(second, (D,), minval=math.log(0.4), maxval=math.log(2.5)))
    return couple(base, col_scale, 0.8).astype(jnp.bfloat16)


def draw_out_grads(key, part):
    key = jax.random.fold_in(key, 2)
    first, second = jax.random.split(key, 2)
    base = jax.random.normal(first, (TOKENS, FFW))
    col_scale = jnp.exp(jax.random.uniform(second, (FFW,), minval=math.log(0.4), maxval=math.log(2.5)))
    return couple(base, col_scale, 0.6).astype(jnp.bfloat16)


def owner_column(key):
    first, second, third = jax.random.split(key, 3)
    ranks = jax.random.permutation(first, N_DP)
    lowest = max(1, NBLK - N_DP)
    highest = NBLK // MOST
    paired = jax.random.randint(second, (), lowest, highest + 1)
    places = jax.random.permutation(third, NBLK)
    position = jnp.arange(NBLK, dtype=jnp.int32)
    group = jnp.where(position < MOST * paired, position // MOST, position - (MOST - 1) * paired)
    values = ranks[group].astype(jnp.int32)
    return jnp.zeros((NBLK,), jnp.int32).at[places].set(values)


def draw_owners(key, part):
    key = jax.random.fold_in(key, 3)
    return jax.vmap(owner_column)(jax.random.split(key, N_MP))


def setup_inputs(seed: int = 0) -> dict:
    arg_keys = jax.random.split(jax.random.key(seed), 4)
    acts = draw_acts(jax.random.fold_in(arg_keys[3], 71), 0)
    out_grads = draw_out_grads(jax.random.fold_in(arg_keys[3], 71), 0)
    owners = draw_owners(jax.random.fold_in(arg_keys[3], 71), 0)
    return dict(acts=acts, out_grads=out_grads, owners=owners)


damping = 0.1

def inverse_root(blocks):
    identity = jnp.eye(blocks.shape[-1], dtype=jnp.float32)
    norms = jnp.sqrt(lax.optimization_barrier(jnp.sum(blocks * blocks, axis=(1, 2))))[:, None, None]
    approx = blocks / norms
    estimate = jnp.broadcast_to(identity, blocks.shape).astype(jnp.float32)

    def advance(index, carry):
        current, guess = carry
        factor = 1.5 * identity - 0.5 * jnp.matmul(guess, current, precision=lax.Precision.HIGHEST)
        return (jnp.matmul(current, factor, precision=lax.Precision.HIGHEST), jnp.matmul(factor, guess, precision=lax.Precision.HIGHEST))
    approx, estimate = lax.fori_loop(0, ITERS, advance, (approx, estimate))
    return (estimate / jnp.sqrt(norms)).astype(jnp.bfloat16)

def block_factor(values, count):
    blocks = values.astype(jnp.float32).reshape(values.shape[0], count, BS)
    summed = jnp.einsum('tbi,tbj->bij', blocks, blocks, precision=lax.Precision.HIGHEST)
    return summed / TOKENS + damping * jnp.eye(BS, dtype=jnp.float32)

def apply_blocks(values, roots):
    count = roots.shape[0]
    blocks = values.astype(jnp.float32).reshape(values.shape[0], count, BS)
    result = jnp.einsum('tbi,bij->tbj', blocks, roots.astype(jnp.float32), precision=lax.Precision.HIGHEST)
    return result.astype(jnp.bfloat16).reshape(values.shape[0], count * BS)

def reference(acts, out_grads, owners):
    aroot = inverse_root(block_factor(acts, D // BS))
    groot = inverse_root(block_factor(out_grads, FFW // BS))
    whitened = apply_blocks(acts, aroot)
    scaled = apply_blocks(out_grads, groot)
    update = jnp.dot(whitened.T, scaled, preferred_element_type=jnp.float32) / jnp.sqrt(jnp.float32(TOKENS))
    ranks = jnp.arange(N_DP, dtype=jnp.int32)
    slots = jnp.arange(MOST, dtype=jnp.int32)
    stacked = []
    for column in range(N_MP):
        roots = jnp.concatenate([aroot[column * DBLK:(column + 1) * DBLK], groot[column * FBLK:(column + 1) * FBLK]], axis=0)
        mine = (owners[column][None, :] == ranks[:, None]).astype(jnp.int32)
        order = jnp.cumsum(mine, axis=1) - 1
        select = (mine[:, None, :] * (order[:, None, :] == slots[None, :, None]).astype(jnp.int32)).astype(jnp.float32)
        stacked.append(jnp.einsum('dsk,kij->dsij', select, roots.astype(jnp.float32), precision=lax.Precision.HIGHEST))
    kept = jnp.stack(stacked, axis=2).reshape(N_DP * MOST, N_MP * BS, BS).astype(jnp.bfloat16)
    return (update.astype(jnp.bfloat16), kept)
```

```python
import functools
import math

import jax
import jax.numpy as jnp
from jax import lax
from jax.experimental import pallas as pl
from jax.experimental.pallas import tpu as pltpu
from jax.sharding import Mesh, PartitionSpec as P

BS = 256
HALF = 128
ITERS = 12
MOST = 2
DAMPING = 0.1
TOKENS = 32768
DP = ("zh", "y", "x", "c")
HIGHEST = lax.Precision.HIGHEST
F32 = jnp.float32
BF16 = jnp.bfloat16


def tdot(lhs, rhs):
    return lax.dot_general(lhs, rhs, (((0,), (0,)), ((), ())), preferred_element_type=F32)


def factor_kernel(where_ref, acts_ref, grads_ref, out_ref):
    step = pl.program_id(0)
    core = where_ref[1]

    def put(slot, block, value):
        for row in range(4):
            out_ref[slot, row, block, 0:64, :] = value[row * 64 : (row + 1) * 64]

    @pl.when(step < 4)
    def _():
        put(core, step, tdot(acts_ref[...], acts_ref[...]))

    @pl.when(jnp.logical_and(step >= 4, step < 8))
    def _():
        put(1 - core, step - 4, tdot(grads_ref[...], grads_ref[...]))

    @pl.when(step == 8)
    def _():
        for half in range(2):
            value = tdot(grads_ref[:, half * HALF : (half + 1) * HALF], grads_ref[...])
            slot = jnp.where(core == half, 0, 1)
            for row in range(4):
                for block in range(4):
                    out_ref[slot, row, block, 64:96, :] = value[row * 32 : (row + 1) * 32]


def factor_parts(where, acts, grads):
    rows = acts.shape[0]
    return pl.pallas_call(
        factor_kernel,
        grid_spec=pltpu.PrefetchScalarGridSpec(
            num_scalar_prefetch=1,
            grid=(9,),
            in_specs=[
                pl.BlockSpec((rows, BS), lambda i, w: (0, w[0] * 4 + jnp.minimum(i, 3))),
                pl.BlockSpec((rows, BS), lambda i, w: (0, jnp.maximum(i - 4, 0))),
            ],
            out_specs=pl.BlockSpec((2, 4, 4, 96, BS), lambda i, w: (0, 0, 0, 0, 0)),
        ),
        out_shape=jax.ShapeDtypeStruct((2, 4, 4, 96, BS), F32),
        compiler_params=pltpu.CompilerParams(vmem_limit_bytes=40 * 2**20),
        cost_estimate=pl.CostEstimate(flops=2 * 9 * rows * BS * BS, bytes_accessed=6 * 2**20, transcendentals=0),
    )(where, acts, grads)


def product_kernel(where_ref, low_ref, high_ref, low_other, high_other, grads_ref, grads_other, out_ref):
    width = grads_ref.shape[1] // 2
    for zh, (mine, other) in enumerate(((low_ref, low_other), (high_ref, high_other))):
        for xl in range(2):
            cols = slice(xl * width, (xl + 1) * width)
            out_ref[0, 0, xl, zh] = tdot(mine[...], grads_ref[:, cols]) + tdot(other[...], grads_other[:, cols])


def product(where, acts, acts_other, grads, grads_other):
    rows, width = grads.shape
    whole = pl.BlockSpec((rows, width), lambda y, h, w: (0, 0))
    return pl.pallas_call(
        product_kernel,
        grid_spec=pltpu.PrefetchScalarGridSpec(
            num_scalar_prefetch=1,
            grid=(4, 2),
            in_specs=[
                pl.BlockSpec((rows, HALF), lambda y, h, w: (0, 2 * (y * 2 + h) + w[1])),
                pl.BlockSpec((rows, HALF), lambda y, h, w: (0, 2 * (8 + y * 2 + h) + w[1])),
                pl.BlockSpec((rows, HALF), lambda y, h, w: (0, y * 2 + h)),
                pl.BlockSpec((rows, HALF), lambda y, h, w: (0, 8 + y * 2 + h)),
                whole,
                whole,
            ],
            out_specs=pl.BlockSpec((1, 1, 2, 2, HALF, width // 2), lambda y, h, w: (y, h, 0, 0, 0, 0)),
        ),
        out_shape=jax.ShapeDtypeStruct((4, 2, 2, 2, HALF, width // 2), F32),
        compiler_params=pltpu.CompilerParams(vmem_limit_bytes=40 * 2**20),
        cost_estimate=pl.CostEstimate(flops=4 * rows * 2048 * width, bytes_accessed=17 * 2**20, transcendentals=0),
    )(where, acts, acts, acts_other, acts_other, grads, grads_other)


def root_kernel(where_ref, block_ref, mine_ref, other_ref, out_ref, last):
    core = where_ref[1]
    last[pl.ds(pl.multiple_of(core * HALF, HALF), HALF), :] = mine_ref[...]
    last[pl.ds(pl.multiple_of((1 - core) * HALF, HALF), HALF), :] = other_ref[...]
    row = lax.broadcasted_iota(jnp.int32, (BS, BS), 0)
    col = lax.broadcasted_iota(jnp.int32, (BS, BS), 1)
    identity = jnp.where(row == col, 1.0, 0.0).astype(F32)
    mul = functools.partial(jnp.dot, precision=HIGHEST, preferred_element_type=F32)

    def start(summed):
        factor = summed * (1.0 / TOKENS) + DAMPING * identity
        norm = jnp.sqrt(jnp.sum(factor * factor, keepdims=True))
        current = factor / norm
        step = 1.5 * identity - 0.5 * current
        return norm, mul(current, step), step

    norm_a, cur_a, est_a = start(block_ref[...])
    norm_b, cur_b, est_b = start(last[...])

    def advance(_, carry):
        cur_a, est_a, cur_b, est_b = carry
        step_a = 1.5 * identity - 0.5 * mul(est_a, cur_a)
        step_b = 1.5 * identity - 0.5 * mul(est_b, cur_b)
        return mul(cur_a, step_a), mul(step_a, est_a), mul(cur_b, step_b), mul(step_b, est_b)

    cur_a, est_a, cur_b, est_b = lax.fori_loop(0, ITERS - 2, advance, (cur_a, est_a, cur_b, est_b))
    step_a = 1.5 * identity - 0.5 * mul(est_a, cur_a)
    step_b = 1.5 * identity - 0.5 * mul(est_b, cur_b)
    out_ref[0] = (mul(step_a, est_a) / jnp.sqrt(norm_a)).astype(BF16)
    out_ref[1] = (mul(step_b, est_b) / jnp.sqrt(norm_b)).astype(BF16)


def two_roots(where, block, mine, other):
    return pl.pallas_call(
        root_kernel,
        grid_spec=pltpu.PrefetchScalarGridSpec(
            num_scalar_prefetch=1,
            grid=(1,),
            in_specs=[
                pl.BlockSpec((BS, BS), lambda i, w: (0, 0)),
                pl.BlockSpec((HALF, BS), lambda i, w: (0, 0)),
                pl.BlockSpec((HALF, BS), lambda i, w: (0, 0)),
            ],
            out_specs=pl.BlockSpec((2, BS, BS), lambda i, w: (0, 0, 0)),
            scratch_shapes=[pltpu.VMEM((BS, BS), F32)],
        ),
        out_shape=jax.ShapeDtypeStruct((2, BS, BS), BF16),
        compiler_params=pltpu.CompilerParams(vmem_limit_bytes=32 * 2**20),
        cost_estimate=pl.CostEstimate(flops=2 * 36 * 6 * 2 * BS**3, bytes_accessed=2**20, transcendentals=0),
    )(where, block, mine, other)


def apply_kernel(where_ref, mine_ref, other_ref, left_ref, right_ref, last_ref, out_ref, rows_ref):
    core = where_ref[1]
    cols = pl.ds(pl.multiple_of(where_ref[2] * HALF, HALF), HALF)

    def side(at, part):
        rows = pl.ds(pl.multiple_of(at * HALF, HALF), HALF)
        return lax.dot_general(
            left_ref[rows, cols].astype(F32), part, (((0,), (0,)), ((), ())), precision=HIGHEST, preferred_element_type=F32
        )

    rows_ref[...] = side(core, mine_ref[...]) + side(1 - core, other_ref[...])
    kept = rows_ref[pl.ds(pl.multiple_of(core * 64, 64), 64), :]
    for block in range(5):
        root = right_ref[block] if block < 4 else last_ref[...]
        span = slice(block * BS, (block + 1) * BS)
        value = jnp.dot(kept[:, span], root.astype(F32), precision=HIGHEST, preferred_element_type=F32)
        out_ref[:, span] = (value * (1.0 / math.sqrt(TOKENS))).astype(BF16)


def apply_roots(where, mine, other, left, right, last):
    width = mine.shape[1]
    return pl.pallas_call(
        apply_kernel,
        grid_spec=pltpu.PrefetchScalarGridSpec(
            num_scalar_prefetch=1,
            grid=(1,),
            in_specs=[
                pl.BlockSpec((HALF, width), lambda i, w: (0, 0)),
                pl.BlockSpec((HALF, width), lambda i, w: (0, 0)),
                pl.BlockSpec((BS, BS), lambda i, w: (0, 0)),
                pl.BlockSpec((4, BS, BS), lambda i, w: (0, 0, 0)),
                pl.BlockSpec((BS, BS), lambda i, w: (0, 0)),
            ],
            out_specs=pl.BlockSpec((64, width), lambda i, w: (0, 0)),
            scratch_shapes=[pltpu.VMEM((HALF, width), F32)],
        ),
        out_shape=jax.ShapeDtypeStruct((64, width), BF16),
        compiler_params=pltpu.CompilerParams(vmem_limit_bytes=32 * 2**20),
        cost_estimate=pl.CostEstimate(flops=12 * 2 * HALF * BS * width, bytes_accessed=3 * 2**20, transcendentals=0),
    )(where, mine, other, left, right, last)


def swap(value, axis):
    return lax.ppermute(value, axis, [(0, 1), (1, 0)])


def per_device(acts, grads, owners):
    zh, y, x, core, column = (lax.axis_index(a) for a in ("zh", "y", "x", "c", "mp"))
    x_high, x_low = x // 2, x % 2
    rows, width = grads.shape
    where = jnp.stack([column, core, x_low]).astype(jnp.int32)

    with jax.named_scope("exchange"):
        halves = acts.reshape(rows, 16, 2, HALF)
        sent = jnp.where(core == 0, halves[:, :, 1], halves[:, :, 0]).reshape(rows, 16 * HALF)
        acts_other = swap(sent, "c")
        grads_other = swap(grads, "c")

    with jax.named_scope("factors"):
        parts = factor_parts(where, acts, grads)
        mine = parts[0] + swap(parts[1], "c")

    with jax.named_scope("product"):
        raw = product(where, acts, acts_other, grads, grads_other)
        raw = raw.reshape(16 * 2 * HALF, width // 2)
        raw = lax.psum_scatter(raw, ("y", "x"), scatter_dimension=0, tiled=True)
        raw = raw.reshape(2, HALF, width // 2)

    with jax.named_scope("sum_factors"):
        mine = lax.all_to_all(mine.reshape(16 * 96, BS), ("y", "x"), 0, 0, tiled=True)
        mine = jnp.sum(mine.reshape(16, 96, BS), axis=0)
        mine = jnp.broadcast_to(mine, (8, 96, BS)).reshape(8 * 96, BS)
        mine = lax.all_to_all(mine, ("zh", "y"), 0, 0, tiled=True).reshape(2, 4, 96, BS)
        mine = mine[0] + mine[1]
        block = mine[:, :64].reshape(BS, BS)
        last_half = mine[:, 64:].reshape(HALF, BS)

    with jax.named_scope("roots"):
        roots = two_roots(where, block, last_half, swap(last_half, "c"))
        last_root = roots[1]
        four = jnp.broadcast_to(roots[0], (4, BS, BS)).reshape(4 * BS, BS)
        four = lax.all_to_all(four, "x", 0, 0, tiled=True).reshape(4, BS, BS)
        other_four = swap(four, "c")
        input_roots = jnp.where(core == 0, four, other_four)
        output_roots = jnp.where(core == 0, other_four, four)

    with jax.named_scope("left_root"):
        holder = zh * 2 + y // 2
        left = lax.dynamic_index_in_dim(input_roots, (y % 2) * 2 + x_high, 0, keepdims=False)
        got = jnp.zeros_like(left)
        for shift in range(1, 4):
            pairs = []
            for a in range(2):
                for b in range(4):
                    source = a * 2 + b // 2
                    pairs.append(((a * 4 + b) * 4 + source, (a * 4 + b) * 4 + (source + shift) % 4))
            got = got + lax.ppermute(left, ("zh", "y", "mp"), pairs)
        left = jnp.where(column == holder, left, got)

    with jax.named_scope("kept"):
        data_rank = ((zh * 4 + y) * 4 + x) * 2 + core
        owned = (owners[0] == data_rank).astype(jnp.int32)
        order = jnp.cumsum(owned) - 1
        slots = jnp.arange(MOST, dtype=jnp.int32)
        select = owned[None, :] * (order[None, :] == slots[:, None]).astype(jnp.int32)
        filled = jnp.sum(select, axis=1)
        place = jnp.argmax(select, axis=1)
        every = jnp.concatenate([input_roots, output_roots, last_root[None]], axis=0)
        kept = jnp.stack(
            [
                jnp.where(filled[s] > 0, lax.dynamic_index_in_dim(every, place[s], 0, keepdims=False), 0).astype(BF16)
                for s in range(MOST)
            ]
        )

    with jax.named_scope("finish"):
        away = lax.dynamic_index_in_dim(raw, 1 - zh, 0, keepdims=False)
        stay = lax.dynamic_index_in_dim(raw, zh, 0, keepdims=False)
        total = stay + swap(away, "zh")
        beside = lax.ppermute(total, "x", [(0, 1), (1, 0), (2, 3), (3, 2)])
        pair = jnp.where(
            x_low == 0, jnp.concatenate([total, beside], axis=1), jnp.concatenate([beside, total], axis=1)
        )
        update = apply_roots(where, pair, swap(pair, "c"), left, output_roots, last_root)
    return update, kept


def solution(mesh):
    fine = Mesh(mesh.devices.reshape(2, 4, 4, 2, 4), ("zh", "y", "x", "c", "mp"))
    return jax.shard_map(
        per_device,
        mesh=fine,
        in_specs=(P(DP, None), P(DP, "mp"), P("mp", None)),
        out_specs=(P(DP, "mp"), P(DP, "mp", None)),
        check_vma=False,
    )
```

```python
import functools
import math

import jax
import jax.numpy as jnp
from jax import lax
from jax.experimental import pallas as pl
from jax.experimental.pallas import tpu as pltpu
from jax.sharding import Mesh, PartitionSpec as P

BS = 256
HALF = 128
ITERS = 12
MOST = 2
DAMPING = 0.1
TOKENS = 32768
DP = ("zh", "y", "x", "c")
HIGHEST = lax.Precision.HIGHEST
F32 = jnp.float32
BF16 = jnp.bfloat16


def tdot(lhs, rhs):
    return lax.dot_general(lhs, rhs, (((0,), (0,)), ((), ())), preferred_element_type=F32)


def factor_kernel(where_ref, acts_ref, grads_ref, out_ref):
    step = pl.program_id(0)
    core = where_ref[1]

    def put(slot, block, value):
        for row in range(4):
            out_ref[slot, row, block, 0:64, :] = value[row * 64 : (row + 1) * 64]

    @pl.when(step < 4)
    def _():
        put(core, step, tdot(acts_ref[...], acts_ref[...]))

    @pl.when(jnp.logical_and(step >= 4, step < 8))
    def _():
        put(1 - core, step - 4, tdot(grads_ref[...], grads_ref[...]))

    @pl.when(step == 8)
    def _():
        for half in range(2):
            value = tdot(grads_ref[:, half * HALF : (half + 1) * HALF], grads_ref[...])
            slot = jnp.where(core == half, 0, 1)
            for row in range(4):
                for block in range(4):
                    out_ref[slot, row, block, 64:96, :] = value[row * 32 : (row + 1) * 32]


def factor_parts(where, acts, grads):
    rows = acts.shape[0]
    return pl.pallas_call(
        factor_kernel,
        grid_spec=pltpu.PrefetchScalarGridSpec(
            num_scalar_prefetch=1,
            grid=(9,),
            in_specs=[
                pl.BlockSpec((rows, BS), lambda i, w: (0, w[0] * 4 + jnp.minimum(i, 3))),
                pl.BlockSpec((rows, BS), lambda i, w: (0, jnp.maximum(i - 4, 0))),
            ],
            out_specs=pl.BlockSpec((2, 4, 4, 96, BS), lambda i, w: (0, 0, 0, 0, 0)),
        ),
        out_shape=jax.ShapeDtypeStruct((2, 4, 4, 96, BS), F32),
        compiler_params=pltpu.CompilerParams(vmem_limit_bytes=40 * 2**20),
        cost_estimate=pl.CostEstimate(flops=2 * 9 * rows * BS * BS, bytes_accessed=6 * 2**20, transcendentals=0),
    )(where, acts, grads)


def product_kernel(where_ref, low_ref, high_ref, low_other, high_other, grads_ref, grads_other, out_ref):
    for zh, (mine, other) in enumerate(((low_ref, low_other), (high_ref, high_other))):
        for xl in range(2):
            cols = slice(xl * HALF, (xl + 1) * HALF)
            out_ref[0, 0, xl, zh] = tdot(mine[:, cols], grads_ref[...]) + tdot(other[:, cols], grads_other[...])


def product(where, acts, acts_other, grads, grads_other):
    rows, width = grads_other.shape
    low = pl.BlockSpec((rows, BS), lambda y, h, w: (0, y * 2 + h))
    high = pl.BlockSpec((rows, BS), lambda y, h, w: (0, 8 + y * 2 + h))
    return pl.pallas_call(
        product_kernel,
        grid_spec=pltpu.PrefetchScalarGridSpec(
            num_scalar_prefetch=1,
            grid=(4, 2),
            in_specs=[
                low,
                high,
                low,
                high,
                pl.BlockSpec((rows, width), lambda y, h, w: (0, w[1])),
                pl.BlockSpec((rows, width), lambda y, h, w: (0, 0)),
            ],
            out_specs=pl.BlockSpec((1, 1, 2, 2, HALF, width), lambda y, h, w: (y, h, 0, 0, 0, 0)),
        ),
        out_shape=jax.ShapeDtypeStruct((4, 2, 2, 2, HALF, width), F32),
        compiler_params=pltpu.CompilerParams(vmem_limit_bytes=40 * 2**20),
        cost_estimate=pl.CostEstimate(flops=4 * rows * 4096 * width, bytes_accessed=20 * 2**20, transcendentals=0),
    )(where, acts, acts, acts_other, acts_other, grads, grads_other)


def root_kernel(where_ref, block_ref, mine_ref, other_ref, out_ref, last):
    core = where_ref[1]
    last[pl.ds(pl.multiple_of(core * HALF, HALF), HALF), :] = mine_ref[...]
    last[pl.ds(pl.multiple_of((1 - core) * HALF, HALF), HALF), :] = other_ref[...]
    row = lax.broadcasted_iota(jnp.int32, (BS, BS), 0)
    col = lax.broadcasted_iota(jnp.int32, (BS, BS), 1)
    identity = jnp.where(row == col, 1.0, 0.0).astype(F32)
    mul = functools.partial(jnp.dot, precision=HIGHEST, preferred_element_type=F32)

    def start(summed):
        factor = summed * (1.0 / TOKENS) + DAMPING * identity
        norm = jnp.sqrt(jnp.sum(factor * factor, keepdims=True))
        current = factor / norm
        step = 1.5 * identity - 0.5 * current
        return norm, mul(current, step), step

    norm_a, cur_a, est_a = start(block_ref[...])
    norm_b, cur_b, est_b = start(last[...])

    def advance(_, carry):
        cur_a, est_a, cur_b, est_b = carry
        step_a = 1.5 * identity - 0.5 * mul(est_a, cur_a)
        step_b = 1.5 * identity - 0.5 * mul(est_b, cur_b)
        return mul(cur_a, step_a), mul(step_a, est_a), mul(cur_b, step_b), mul(step_b, est_b)

    cur_a, est_a, cur_b, est_b = lax.fori_loop(0, ITERS - 2, advance, (cur_a, est_a, cur_b, est_b))
    step_a = 1.5 * identity - 0.5 * mul(est_a, cur_a)
    step_b = 1.5 * identity - 0.5 * mul(est_b, cur_b)
    out_ref[0] = (mul(step_a, est_a) / jnp.sqrt(norm_a)).astype(BF16)
    out_ref[1] = (mul(step_b, est_b) / jnp.sqrt(norm_b)).astype(BF16)


def two_roots(where, block, mine, other):
    return pl.pallas_call(
        root_kernel,
        grid_spec=pltpu.PrefetchScalarGridSpec(
            num_scalar_prefetch=1,
            grid=(1,),
            in_specs=[
                pl.BlockSpec((BS, BS), lambda i, w: (0, 0)),
                pl.BlockSpec((HALF, BS), lambda i, w: (0, 0)),
                pl.BlockSpec((HALF, BS), lambda i, w: (0, 0)),
            ],
            out_specs=pl.BlockSpec((2, BS, BS), lambda i, w: (0, 0, 0)),
            scratch_shapes=[pltpu.VMEM((BS, BS), F32)],
        ),
        out_shape=jax.ShapeDtypeStruct((2, BS, BS), BF16),
        compiler_params=pltpu.CompilerParams(vmem_limit_bytes=32 * 2**20),
        cost_estimate=pl.CostEstimate(flops=2 * 36 * 6 * 2 * BS**3, bytes_accessed=2**20, transcendentals=0),
    )(where, block, mine, other)


def apply_kernel(where_ref, mine_ref, beside_ref, mine_other, beside_other, left_ref, right_ref, last_ref, out_ref, rows_ref):
    core, x_low = where_ref[1], where_ref[2]
    width = mine_ref.shape[1]
    cols = pl.ds(pl.multiple_of(x_low * HALF, HALF), HALF)

    def side(at, part):
        rows = pl.ds(pl.multiple_of(at * HALF, HALF), HALF)
        return lax.dot_general(
            left_ref[rows, cols].astype(F32), part, (((0,), (0,)), ((), ())), precision=HIGHEST, preferred_element_type=F32
        )

    for at, mine, beside in ((core, mine_ref, beside_ref), (1 - core, mine_other, beside_other)):
        span = pl.ds(pl.multiple_of(at * width, HALF), width)
        rows_ref[:, span] = side(x_low, mine[...]) + side(1 - x_low, beside[...])
    kept = rows_ref[pl.ds(pl.multiple_of(core * 64, 64), 64), :]
    for block in range(5):
        root = right_ref[block] if block < 4 else last_ref[...]
        span = slice(block * BS, (block + 1) * BS)
        value = jnp.dot(kept[:, span], root.astype(F32), precision=HIGHEST, preferred_element_type=F32)
        out_ref[:, span] = (value * (1.0 / math.sqrt(TOKENS))).astype(BF16)


def apply_roots(where, pieces, left, right, last):
    width = pieces[0].shape[1]
    piece = pl.BlockSpec((HALF, width), lambda i, w: (0, 0))
    return pl.pallas_call(
        apply_kernel,
        grid_spec=pltpu.PrefetchScalarGridSpec(
            num_scalar_prefetch=1,
            grid=(1,),
            in_specs=[
                piece,
                piece,
                piece,
                piece,
                pl.BlockSpec((BS, BS), lambda i, w: (0, 0)),
                pl.BlockSpec((4, BS, BS), lambda i, w: (0, 0, 0)),
                pl.BlockSpec((BS, BS), lambda i, w: (0, 0)),
            ],
            out_specs=pl.BlockSpec((64, 2 * width), lambda i, w: (0, 0)),
            scratch_shapes=[pltpu.VMEM((HALF, 2 * width), F32)],
        ),
        out_shape=jax.ShapeDtypeStruct((64, 2 * width), BF16),
        compiler_params=pltpu.CompilerParams(vmem_limit_bytes=32 * 2**20),
        cost_estimate=pl.CostEstimate(flops=12 * 4 * HALF * BS * width, bytes_accessed=3 * 2**20, transcendentals=0),
    )(where, *pieces, left, right, last)


def swap(value, axis):
    return lax.ppermute(value, axis, [(0, 1), (1, 0)])


def per_device(acts, grads, owners):
    zh, y, x, core, column = (lax.axis_index(a) for a in ("zh", "y", "x", "c", "mp"))
    x_high, x_low = x // 2, x % 2
    rows, width = grads.shape
    where = jnp.stack([column, core, x_low]).astype(jnp.int32)

    with jax.named_scope("exchange"):
        acts_other = swap(acts, "c")
        sent = lax.dynamic_slice_in_dim(grads, (1 - core) * (width // 2), width // 2, 1)
        grads_other = swap(sent, "c")

    with jax.named_scope("factors"):
        parts = factor_parts(where, acts, grads)
        mine = parts[0] + swap(parts[1], "c")

    with jax.named_scope("product"):
        raw = product(where, acts, acts_other, grads, grads_other)
        raw = raw.reshape(16 * 2 * HALF, width // 2)
        raw = lax.psum_scatter(raw, ("y", "x"), scatter_dimension=0, tiled=True)
        raw = raw.reshape(2, HALF, width // 2)

    with jax.named_scope("sum_factors"):
        mine = lax.all_to_all(mine.reshape(16 * 96, BS), ("y", "x"), 0, 0, tiled=True)
        mine = jnp.sum(mine.reshape(16, 96, BS), axis=0)
        mine = jnp.broadcast_to(mine, (8, 96, BS)).reshape(8 * 96, BS)
        mine = lax.all_to_all(mine, ("zh", "y"), 0, 0, tiled=True).reshape(2, 4, 96, BS)
        mine = mine[0] + mine[1]
        block = mine[:, :64].reshape(BS, BS)
        last_half = mine[:, 64:].reshape(HALF, BS)

    with jax.named_scope("roots"):
        roots = two_roots(where, block, last_half, swap(last_half, "c"))
        last_root = roots[1]
        four = jnp.broadcast_to(roots[0], (4, BS, BS)).reshape(4 * BS, BS)
        four = lax.all_to_all(four, "x", 0, 0, tiled=True).reshape(4, BS, BS)
        other_four = swap(four, "c")
        input_roots = jnp.where(core == 0, four, other_four)
        output_roots = jnp.where(core == 0, other_four, four)

    with jax.named_scope("left_root"):
        holder = zh * 2 + y // 2
        left = lax.dynamic_index_in_dim(input_roots, (y % 2) * 2 + x_high, 0, keepdims=False)
        got = jnp.zeros_like(left)
        for shift in range(1, 4):
            pairs = []
            for a in range(2):
                for b in range(4):
                    source = a * 2 + b // 2
                    pairs.append(((a * 4 + b) * 4 + source, (a * 4 + b) * 4 + (source + shift) % 4))
            got = got + lax.ppermute(left, ("zh", "y", "mp"), pairs)
        left = jnp.where(column == holder, left, got)

    with jax.named_scope("kept"):
        data_rank = ((zh * 4 + y) * 4 + x) * 2 + core
        owned = (owners[0] == data_rank).astype(jnp.int32)
        order = jnp.cumsum(owned) - 1
        slots = jnp.arange(MOST, dtype=jnp.int32)
        select = owned[None, :] * (order[None, :] == slots[:, None]).astype(jnp.int32)
        filled = jnp.sum(select, axis=1)
        place = jnp.argmax(select, axis=1)
        every = jnp.concatenate([input_roots, output_roots, last_root[None]], axis=0)
        kept = jnp.stack(
            [
                jnp.where(filled[s] > 0, lax.dynamic_index_in_dim(every, place[s], 0, keepdims=False), 0).astype(BF16)
                for s in range(MOST)
            ]
        )

    with jax.named_scope("finish"):
        raw, left = lax.optimization_barrier((raw, left))
        away = lax.dynamic_index_in_dim(raw, 1 - zh, 0, keepdims=False)
        stay = lax.dynamic_index_in_dim(raw, zh, 0, keepdims=False)
        total = stay + swap(away, "zh")
        beside = lax.ppermute(total, "x", [(0, 1), (1, 0), (2, 3), (3, 2)])
        pieces = (total, beside, swap(total, "c"), swap(beside, "c"))
        update = apply_roots(where, pieces, left, output_roots, last_root)
    return update, kept


def solution(mesh):
    fine = Mesh(mesh.devices.reshape(2, 4, 4, 2, 4), ("zh", "y", "x", "c", "mp"))
    return jax.shard_map(
        per_device,
        mesh=fine,
        in_specs=(P(DP, None), P(DP, "mp"), P("mp", None)),
        out_specs=(P(DP, "mp"), P(DP, "mp", None)),
        check_vma=False,
    )
```

```python
import functools
import math

import jax
import jax.numpy as jnp
from jax import lax
from jax.experimental import pallas as pl
from jax.experimental.pallas import tpu as pltpu
from jax.sharding import Mesh, PartitionSpec as P

BS = 256
HALF = 128
ITERS = 12
MOST = 2
DAMPING = 0.1
TOKENS = 32768
DP = ("zh", "y", "x", "c")
HIGHEST = lax.Precision.HIGHEST
F32 = jnp.float32
BF16 = jnp.bfloat16


def tdot(lhs, rhs):
    return lax.dot_general(lhs, rhs, (((0,), (0,)), ((), ())), preferred_element_type=F32)


def factor_kernel(where_ref, acts_ref, grads_ref, out_ref):
    step = pl.program_id(0)
    core = where_ref[1]

    def put(slot, block, value):
        for row in range(4):
            out_ref[slot, row, block, 0:64, :] = value[row * 64 : (row + 1) * 64]

    @pl.when(step < 4)
    def _():
        put(core, step, tdot(acts_ref[...], acts_ref[...]))

    @pl.when(jnp.logical_and(step >= 4, step < 8))
    def _():
        put(1 - core, step - 4, tdot(grads_ref[...], grads_ref[...]))

    @pl.when(step == 8)
    def _():
        for half in range(2):
            value = tdot(grads_ref[:, half * HALF : (half + 1) * HALF], grads_ref[...])
            slot = jnp.where(core == half, 0, 1)
            for row in range(4):
                for block in range(4):
                    out_ref[slot, row, block, 64:96, :] = value[row * 32 : (row + 1) * 32]


def factor_parts(where, acts, grads):
    rows = acts.shape[0]
    return pl.pallas_call(
        factor_kernel,
        grid_spec=pltpu.PrefetchScalarGridSpec(
            num_scalar_prefetch=1,
            grid=(9,),
            in_specs=[
                pl.BlockSpec((rows, BS), lambda i, w: (0, w[0] * 4 + jnp.minimum(i, 3))),
                pl.BlockSpec((rows, BS), lambda i, w: (0, jnp.maximum(i - 4, 0))),
            ],
            out_specs=pl.BlockSpec((2, 4, 4, 96, BS), lambda i, w: (0, 0, 0, 0, 0)),
        ),
        out_shape=jax.ShapeDtypeStruct((2, 4, 4, 96, BS), F32),
        compiler_params=pltpu.CompilerParams(vmem_limit_bytes=40 * 2**20),
        cost_estimate=pl.CostEstimate(flops=2 * 9 * rows * BS * BS, bytes_accessed=6 * 2**20, transcendentals=0),
    )(where, acts, grads)


def product_kernel(where_ref, a_mine, a_other, b_mine, b_other, grads_ref, grads_other, a_out, b_out):
    a_out[0] = tdot(a_mine[...], grads_ref[...]) + tdot(a_other[...], grads_other[...])
    b_out[0] = tdot(b_mine[...], grads_ref[...]) + tdot(b_other[...], grads_other[...])


def product(where, shift, acts, acts_other, grads, grads_other):
    rows, width = grads_other.shape
    first = pl.BlockSpec((rows, HALF), lambda j, w: (0, 4 * j + lax.rem(w[3] + shift, 4)))
    second = pl.BlockSpec((rows, HALF), lambda j, w: (0, 16 + 4 * lax.rem(w[4] + shift, 4) + j))
    out = pl.BlockSpec((1, HALF, width), lambda j, w: (j, 0, 0))
    shape = jax.ShapeDtypeStruct((4, HALF, width), F32)
    return pl.pallas_call(
        product_kernel,
        grid_spec=pltpu.PrefetchScalarGridSpec(
            num_scalar_prefetch=1,
            grid=(4,),
            in_specs=[
                first,
                first,
                second,
                second,
                pl.BlockSpec((rows, width), lambda j, w: (0, w[1])),
                pl.BlockSpec((rows, width), lambda j, w: (0, 0)),
            ],
            out_specs=[out, out],
        ),
        out_shape=[shape, shape],
        compiler_params=pltpu.CompilerParams(vmem_limit_bytes=24 * 2**20),
        cost_estimate=pl.CostEstimate(flops=4 * rows * 1024 * width, bytes_accessed=6 * 2**20, transcendentals=0),
    )(where, acts, acts_other, acts, acts_other, grads, grads_other)


def root_kernel(where_ref, block_ref, mine_ref, other_ref, out_ref, last):
    core = where_ref[1]
    last[pl.ds(pl.multiple_of(core * HALF, HALF), HALF), :] = mine_ref[...]
    last[pl.ds(pl.multiple_of((1 - core) * HALF, HALF), HALF), :] = other_ref[...]
    row = lax.broadcasted_iota(jnp.int32, (BS, BS), 0)
    col = lax.broadcasted_iota(jnp.int32, (BS, BS), 1)
    identity = jnp.where(row == col, 1.0, 0.0).astype(F32)
    mul = functools.partial(jnp.dot, precision=HIGHEST, preferred_element_type=F32)

    def start(summed):
        factor = summed * (1.0 / TOKENS) + DAMPING * identity
        norm = jnp.sqrt(jnp.sum(factor * factor, keepdims=True))
        current = factor / norm
        step = 1.5 * identity - 0.5 * current
        return norm, mul(current, step), step

    norm_a, cur_a, est_a = start(block_ref[...])
    norm_b, cur_b, est_b = start(last[...])

    def advance(_, carry):
        cur_a, est_a, cur_b, est_b = carry
        step_a = 1.5 * identity - 0.5 * mul(est_a, cur_a)
        step_b = 1.5 * identity - 0.5 * mul(est_b, cur_b)
        return mul(cur_a, step_a), mul(step_a, est_a), mul(cur_b, step_b), mul(step_b, est_b)

    cur_a, est_a, cur_b, est_b = lax.fori_loop(0, ITERS - 2, advance, (cur_a, est_a, cur_b, est_b))
    step_a = 1.5 * identity - 0.5 * mul(est_a, cur_a)
    step_b = 1.5 * identity - 0.5 * mul(est_b, cur_b)
    out_ref[0] = (mul(step_a, est_a) / jnp.sqrt(norm_a)).astype(BF16)
    out_ref[1] = (mul(step_b, est_b) / jnp.sqrt(norm_b)).astype(BF16)


def two_roots(where, block, mine, other):
    return pl.pallas_call(
        root_kernel,
        grid_spec=pltpu.PrefetchScalarGridSpec(
            num_scalar_prefetch=1,
            grid=(1,),
            in_specs=[
                pl.BlockSpec((BS, BS), lambda i, w: (0, 0)),
                pl.BlockSpec((HALF, BS), lambda i, w: (0, 0)),
                pl.BlockSpec((HALF, BS), lambda i, w: (0, 0)),
            ],
            out_specs=pl.BlockSpec((2, BS, BS), lambda i, w: (0, 0, 0)),
            scratch_shapes=[pltpu.VMEM((BS, BS), F32)],
        ),
        out_shape=jax.ShapeDtypeStruct((2, BS, BS), BF16),
        compiler_params=pltpu.CompilerParams(vmem_limit_bytes=32 * 2**20),
        cost_estimate=pl.CostEstimate(flops=2 * 36 * 6 * 2 * BS**3, bytes_accessed=2**20, transcendentals=0),
    )(where, block, mine, other)


def apply_kernel(where_ref, mine_ref, beside_ref, mine_other, beside_other, left_ref, right_ref, last_ref, out_ref, rows_ref):
    core, x_low = where_ref[1], where_ref[2]
    width = mine_ref.shape[1]
    cols = pl.ds(pl.multiple_of(x_low * HALF, HALF), HALF)

    def side(at, part):
        rows = pl.ds(pl.multiple_of(at * HALF, HALF), HALF)
        return lax.dot_general(
            left_ref[rows, cols].astype(F32), part, (((0,), (0,)), ((), ())), precision=HIGHEST, preferred_element_type=F32
        )

    for at, mine, beside in ((core, mine_ref, beside_ref), (1 - core, mine_other, beside_other)):
        span = pl.ds(pl.multiple_of(at * width, HALF), width)
        rows_ref[:, span] = side(x_low, mine[...]) + side(1 - x_low, beside[...])
    kept = rows_ref[pl.ds(pl.multiple_of(core * 64, 64), 64), :]
    for block in range(5):
        root = right_ref[block] if block < 4 else last_ref[...]
        span = slice(block * BS, (block + 1) * BS)
        value = jnp.dot(kept[:, span], root.astype(F32), precision=HIGHEST, preferred_element_type=F32)
        out_ref[:, span] = (value * (1.0 / math.sqrt(TOKENS))).astype(BF16)


def apply_roots(where, pieces, left, right, last):
    width = pieces[0].shape[1]
    piece = pl.BlockSpec((HALF, width), lambda i, w: (0, 0))
    return pl.pallas_call(
        apply_kernel,
        grid_spec=pltpu.PrefetchScalarGridSpec(
            num_scalar_prefetch=1,
            grid=(1,),
            in_specs=[
                piece,
                piece,
                piece,
                piece,
                pl.BlockSpec((BS, BS), lambda i, w: (0, 0)),
                pl.BlockSpec((4, BS, BS), lambda i, w: (0, 0, 0)),
                pl.BlockSpec((BS, BS), lambda i, w: (0, 0)),
            ],
            out_specs=pl.BlockSpec((64, 2 * width), lambda i, w: (0, 0)),
            scratch_shapes=[pltpu.VMEM((HALF, 2 * width), F32)],
        ),
        out_shape=jax.ShapeDtypeStruct((64, 2 * width), BF16),
        compiler_params=pltpu.CompilerParams(vmem_limit_bytes=32 * 2**20),
        cost_estimate=pl.CostEstimate(flops=12 * 4 * HALF * BS * width, bytes_accessed=3 * 2**20, transcendentals=0),
    )(where, *pieces, left, right, last)


def swap(value, axis):
    return lax.ppermute(value, axis, [(0, 1), (1, 0)])


def away(value, axis, shift):
    if shift == 0:
        return value
    return lax.ppermute(value, axis, [(i, (i + shift) % 4) for i in range(4)])


def across(value, axis, at):
    parts = [
        away(lax.dynamic_index_in_dim(value, lax.rem(at + shift, 4), 0, keepdims=False), axis, shift)
        for shift in (2, 1, 3, 0)
    ]
    return (parts[3] + parts[0]) + (parts[1] + parts[2])


def per_device(acts, grads, owners):
    zh, y, x, core, column = (lax.axis_index(a) for a in ("zh", "y", "x", "c", "mp"))
    x_high, x_low = x // 2, x % 2
    rows, width = grads.shape
    where = jnp.stack([column, core, x_low, x, y]).astype(jnp.int32)

    with jax.named_scope("exchange"):
        acts_other = swap(acts, "c")
        sent = lax.dynamic_slice_in_dim(grads, (1 - core) * (width // 2), width // 2, 1)
        grads_other = swap(sent, "c")

    with jax.named_scope("factors"):
        parts = factor_parts(where, acts, grads)
        mine = parts[0] + swap(parts[1], "c")

    with jax.named_scope("product"):
        first, second = [], []
        for shift in (2, 1, 3, 0):
            one, two = product(where, shift, acts, acts_other, grads, grads_other)
            first.append(away(one, "x", shift))
            second.append(away(two, "y", shift))

    with jax.named_scope("sum_factors"):
        mine = lax.all_to_all(mine.reshape(16 * 96, BS), ("y", "x"), 0, 0, tiled=True)
        mine = jnp.sum(mine.reshape(16, 96, BS), axis=0)
        mine = jnp.broadcast_to(mine, (8, 96, BS)).reshape(8 * 96, BS)
        mine = lax.all_to_all(mine, ("zh", "y"), 0, 0, tiled=True).reshape(2, 4, 96, BS)
        mine = mine[0] + mine[1]
        block = mine[:, :64].reshape(BS, BS)
        last_half = mine[:, 64:].reshape(HALF, BS)

    with jax.named_scope("roots"):
        roots = two_roots(where, block, last_half, swap(last_half, "c"))
        last_root = roots[1]
        four = jnp.broadcast_to(roots[0], (4, BS, BS)).reshape(4 * BS, BS)
        four = lax.all_to_all(four, "x", 0, 0, tiled=True).reshape(4, BS, BS)
        other_four = swap(four, "c")
        input_roots = jnp.where(core == 0, four, other_four)
        output_roots = jnp.where(core == 0, other_four, four)

    with jax.named_scope("left_root"):
        holder = zh * 2 + y // 2
        left = lax.dynamic_index_in_dim(input_roots, (y % 2) * 2 + x_high, 0, keepdims=False)
        got = jnp.zeros_like(left)
        for shift in range(1, 4):
            pairs = []
            for a in range(2):
                for b in range(4):
                    source = a * 2 + b // 2
                    pairs.append(((a * 4 + b) * 4 + source, (a * 4 + b) * 4 + (source + shift) % 4))
            got = got + lax.ppermute(left, ("zh", "y", "mp"), pairs)
        left = jnp.where(column == holder, left, got)

    with jax.named_scope("kept"):
        data_rank = ((zh * 4 + y) * 4 + x) * 2 + core
        owned = (owners[0] == data_rank).astype(jnp.int32)
        order = jnp.cumsum(owned) - 1
        slots = jnp.arange(MOST, dtype=jnp.int32)
        select = owned[None, :] * (order[None, :] == slots[:, None]).astype(jnp.int32)
        filled = jnp.sum(select, axis=1)
        place = jnp.argmax(select, axis=1)
        every = jnp.concatenate([input_roots, output_roots, last_root[None]], axis=0)
        kept = jnp.stack(
            [
                jnp.where(filled[s] > 0, lax.dynamic_index_in_dim(every, place[s], 0, keepdims=False), 0).astype(BF16)
                for s in range(MOST)
            ]
        )

    with jax.named_scope("finish"):
        low = across((first[3] + first[0]) + (first[1] + first[2]), "y", y)
        high = across((second[3] + second[0]) + (second[1] + second[2]), "x", x)
        stay = jnp.where(zh == 0, low, high)
        total = stay + swap(jnp.where(zh == 0, high, low), "zh")
        beside = lax.ppermute(total, "x", [(0, 1), (1, 0), (2, 3), (3, 2)])
        pieces = (total, beside, swap(total, "c"), swap(beside, "c"))
        update = apply_roots(where, pieces, left, output_roots, last_root)
    return update, kept


def solution(mesh):
    fine = Mesh(mesh.devices.reshape(2, 4, 4, 2, 4), ("zh", "y", "x", "c", "mp"))
    return jax.shard_map(
        per_device,
        mesh=fine,
        in_specs=(P(DP, None), P(DP, "mp"), P("mp", None)),
        out_specs=(P(DP, "mp"), P(DP, "mp", None)),
        check_vma=False,
    )
```

```python
import functools
import math

import jax
import jax.numpy as jnp
from jax import lax
from jax.experimental import pallas as pl
from jax.experimental.pallas import tpu as pltpu
from jax.sharding import Mesh, PartitionSpec as P

BS = 256
HALF = 128
ITERS = 12
MOST = 2
DAMPING = 0.1
TOKENS = 32768
DP = ("zh", "y", "x", "c")
HIGHEST = lax.Precision.HIGHEST
F32 = jnp.float32
BF16 = jnp.bfloat16


def tdot(lhs, rhs):
    return lax.dot_general(lhs, rhs, (((0,), (0,)), ((), ())), preferred_element_type=F32)


SMEM = pl.BlockSpec(memory_space=pltpu.SMEM)
ANY = pl.BlockSpec(memory_space=pl.ANY)
SHIFTS = (2, 1, 3, 0)


def at(start, size, step=HALF):
    return pl.ds(pl.multiple_of(start, step), size)


def whole(array):
    return pl.BlockSpec(array.shape, lambda *_: (0,) * len(array.shape))


def call(kernel, grid, scalars, in_specs, out_specs, out_shape, operands, scratch=(), limit=60, flops=0):
    return pl.pallas_call(
        kernel,
        grid_spec=pltpu.PrefetchScalarGridSpec(
            num_scalar_prefetch=1, grid=grid, in_specs=in_specs, out_specs=out_specs, scratch_shapes=scratch
        ),
        out_shape=out_shape,
        compiler_params=pltpu.CompilerParams(vmem_limit_bytes=limit * 2**20),
        cost_estimate=pl.CostEstimate(flops=flops, bytes_accessed=2**18, transcendentals=0),
    )(scalars, *operands)


def factor_kernel(where_ref, acts_ref, grads_ref, kept_ref, sent_ref):
    def write(out_ref, ref, half):
        for block in range(4):
            span = ref[:, block * BS : (block + 1) * BS]
            value = tdot(span, span)
            for row in range(4):
                out_ref[row, block, 0:64, :] = value[row * 64 : (row + 1) * 64]
        value = tdot(grads_ref[:, 4 * BS + half * HALF : 4 * BS + (half + 1) * HALF], grads_ref[:, 4 * BS :])
        for row in range(4):
            for block in range(4):
                out_ref[row, block, 64:96, :] = value[row * 32 : (row + 1) * 32]

    @pl.when(where_ref[1] == 0)
    def _():
        write(kept_ref, acts_ref, 0)
        write(sent_ref, grads_ref, 1)

    @pl.when(where_ref[1] == 1)
    def _():
        write(sent_ref, acts_ref, 0)
        write(kept_ref, grads_ref, 1)


def factor_parts(where, acts, grads):
    rows = acts.shape[0]
    shape = jax.ShapeDtypeStruct((4, 4, 96, BS), F32)
    return call(
        factor_kernel,
        (1,),
        where,
        [pl.BlockSpec((rows, 4 * BS), lambda i, w: (0, w[0])), whole(grads)],
        [whole(shape)] * 2,
        [shape] * 2,
        (acts, grads),
    )


def multiply_all(mine, other, grads_ref, grads_other):
    def multiply(left, right):
        return tdot(grads_ref[...], left) + tdot(grads_other[...], right)

    return (
        multiply(jnp.concatenate([r[...] for r in mine[:4]], axis=1), jnp.concatenate([r[...] for r in other[:4]], axis=1)),
        multiply(mine[4][...], other[4][...]),
    )


def far_kernel(where_ref, *refs):
    for part, value in enumerate(multiply_all(refs[0:5], refs[5:10], refs[10], refs[11])):
        for j in range(4):
            refs[13 + part * 2 + j // 2][j % 2] = value[:, j * HALF : (j + 1) * HALF]


def near_kernel(where_ref, *refs):
    outs, slots, sems = refs[13:17], refs[17], refs[18]
    step = pl.program_id(0)

    def copies(k):
        return [pltpu.make_async_copy(slots.at[k, part], outs[part * 2 + k], sems.at[k, part]) for part in range(2)]

    for k in range(2):

        @pl.when(step == k)
        def _(k=k):
            for part, value in enumerate(multiply_all(refs[0:5], refs[5:10], refs[10], refs[11])):
                for j in range(4):
                    slots[k, part, j] = value[:, j * HALF : (j + 1) * HALF]
            for copy in copies(k):
                copy.start()

    @pl.when(step == 1)
    def _():
        for k in range(2):
            for copy in copies(k):
                copy.wait()


def home_kernel(where_ref, *refs):
    for value, out in zip(multiply_all(refs[0:5], refs[5:10], refs[10], refs[11]), refs[13:15], strict=True):
        for j in range(4):
            out[j] = value[:, j * HALF : (j + 1) * HALF]


def product(kernel, where, shifts, acts, acts_other, grads, grads_other, earlier, out_specs, out_shape, **more):
    rows, width = grads.shape[0], grads.shape[1] // 2

    def there(place, i):
        shift = shifts[0]
        for k in range(1, len(shifts)):
            shift = jnp.where(i == k, shifts[k], shift)
        return lax.rem(place + shift, 4)

    lefts = [
        pl.BlockSpec((rows, HALF), functools.partial(lambda j, i, w: (0, 4 * j + there(w[3], i)), j)) for j in range(4)
    ] + [pl.BlockSpec((rows, 4 * HALF), lambda i, w: (0, 4 + there(w[4], i)))]
    columns = pl.BlockSpec((rows, width), lambda i, w: (0, w[1]))
    return call(
        kernel,
        (len(shifts),),
        where,
        lefts + lefts + [columns, columns, ANY],
        out_specs,
        out_shape,
        [acts] * 5 + [acts_other] * 5 + [grads, grads_other, earlier],
        **more,
    )


def far_products(where, *inputs):
    two = jax.ShapeDtypeStruct((2, inputs[2].shape[1] // 2, HALF), F32)
    return product(far_kernel, where, (2,), *inputs, [whole(two)] * 4, [two] * 4)


def near_products(where, *inputs):
    width = inputs[2].shape[1] // 2
    four = jax.ShapeDtypeStruct((4, width, HALF), F32)
    scratch = [pltpu.VMEM((2, 2, 4, width, HALF), F32), pltpu.SemaphoreType.DMA((2, 2))]
    return product(near_kernel, where, (1, 3), *inputs, [ANY] * 4, [four] * 4, scratch=scratch)


def home_products(where, *inputs):
    four = jax.ShapeDtypeStruct((4, inputs[2].shape[1] // 2, HALF), F32)
    return product(home_kernel, where, (0,), *inputs, [whole(four)] * 2, [four] * 2)


def merge_kernel(_, *refs):
    for k in range(4):
        refs[9 + k][...] = refs[k][...] + refs[4 + k][...]


def merge(where, near, came, earlier):
    shape = near[0].shape
    block = (1, *shape[1:])
    low = pl.BlockSpec(block, lambda i, w: (i, 0, 0))
    high = pl.BlockSpec(block, lambda i, w: (2 + i, 0, 0))
    return pl.pallas_call(
        merge_kernel,
        grid_spec=pltpu.PrefetchScalarGridSpec(
            num_scalar_prefetch=1,
            grid=(2,),
            in_specs=[low, high, low, high] + [low] * 4 + [ANY],
            out_specs=[low, high, low, high],
        ),
        out_shape=[jax.ShapeDtypeStruct(shape, F32)] * 4,
        input_output_aliases={1: 0, 2: 1, 3: 2, 4: 3},
        compiler_params=pltpu.CompilerParams(vmem_limit_bytes=60 * 2**20),
        cost_estimate=pl.CostEstimate(flops=0, bytes_accessed=2**18, transcendentals=0),
    )(where, *near, *came, earlier)


def route_kernel(_, *refs):
    for part in range(2):
        own, below, above = refs[part * 3 : part * 3 + 3]
        refs[7 + part][...] = own[...] + (below[...] + above[...])


def route(where, first, second, earlier):
    shape = jax.ShapeDtypeStruct(first[0].shape, F32)
    every = pl.BlockSpec((1, *shape.shape[1:]), lambda i, w: (i, 0, 0))
    return call(
        route_kernel, (4,), where, [every] * 6 + [ANY], [every] * 2, [shape] * 2, (*first, *second, earlier)
    )


def settle_kernel(where_ref, low_ref, h0, h1, h2, h3, _, stay_ref, leave_ref):
    low = (low_ref[0] + low_ref[1]) + (low_ref[2] + low_ref[3])
    high = (h3[...] + h0[...]) + (h1[...] + h2[...])

    @pl.when(where_ref[5] == 0)
    def _():
        stay_ref[...] = low
        leave_ref[...] = high

    @pl.when(where_ref[5] == 1)
    def _():
        stay_ref[...] = high
        leave_ref[...] = low


def settle(where, low, high, earlier):
    shape = jax.ShapeDtypeStruct(low.shape[1:], F32)
    specs = [whole(low)] + [whole(shape)] * 4 + [ANY]
    return call(settle_kernel, (1,), where, specs, [whole(shape)] * 2, [shape] * 2, (low, *high, earlier), limit=16)


def fold_kernel(_, in_ref, out_ref):
    rows = out_ref.shape[0]
    total = in_ref[0:rows]
    for source in range(1, 16):
        total = total + in_ref[source * rows : (source + 1) * rows]
    out_ref[...] = total


def fold(where, parts):
    shape = jax.ShapeDtypeStruct((parts.shape[0] // 16, BS), F32)
    return call(fold_kernel, (1,), where, [whole(parts)], whole(shape), shape, (parts,), limit=16)


def root_kernel(where_ref, p0, p1, p2, p3, _, out_ref, block_ref, last):
    core = where_ref[1]
    for shift, piece in enumerate((p0, p1, p2, p3)):
        place = lax.rem(where_ref[4] + 4 - shift, 4)
        block_ref[at(place * 64, 64, 64), :] = piece[0:64]
        last[at(core * HALF + place * 32, 32, 32), :] = piece[64:96]
        last[at((1 - core) * HALF + place * 32, 32, 32), :] = piece[96:128]
    row = lax.broadcasted_iota(jnp.int32, (BS, BS), 0)
    col = lax.broadcasted_iota(jnp.int32, (BS, BS), 1)
    identity = jnp.where(row == col, 1.0, 0.0).astype(F32)
    mul = functools.partial(jnp.dot, precision=HIGHEST, preferred_element_type=F32)

    def start(summed):
        factor = summed * (1.0 / TOKENS) + DAMPING * identity
        norm = jnp.sqrt(jnp.sum(factor * factor, keepdims=True))
        current = factor / norm
        step = 1.5 * identity - 0.5 * current
        return norm, mul(current, step), step

    norm_a, cur_a, est_a = start(block_ref[...])
    norm_b, cur_b, est_b = start(last[...])

    def advance(_, carry):
        cur_a, est_a, cur_b, est_b = carry
        step_a = 1.5 * identity - 0.5 * mul(est_a, cur_a)
        step_b = 1.5 * identity - 0.5 * mul(est_b, cur_b)
        return mul(cur_a, step_a), mul(step_a, est_a), mul(cur_b, step_b), mul(step_b, est_b)

    cur_a, est_a, cur_b, est_b = lax.fori_loop(0, ITERS - 2, advance, (cur_a, est_a, cur_b, est_b))
    step_a = 1.5 * identity - 0.5 * mul(est_a, cur_a)
    step_b = 1.5 * identity - 0.5 * mul(est_b, cur_b)
    out_ref[0] = (mul(step_a, est_a) / jnp.sqrt(norm_a)).astype(BF16)
    out_ref[1] = (mul(step_b, est_b) / jnp.sqrt(norm_b)).astype(BF16)


def two_roots(where, pieces, earlier):
    shape = jax.ShapeDtypeStruct((2, BS, BS), BF16)
    return call(
        root_kernel,
        (1,),
        where,
        [whole(p) for p in pieces] + [ANY],
        whole(shape),
        shape,
        (*pieces, earlier),
        scratch=[pltpu.VMEM((BS, BS), F32), pltpu.VMEM((BS, BS), F32)],
        limit=32,
    )


def apply_kernel(where_ref, mine_ref, beside_ref, mine_other, beside_other, left_ref, right_ref, last_ref, out_ref, left_done, done):
    core, x_low = where_ref[1], where_ref[2]
    width = mine_ref.shape[0]
    cols = at(x_low * HALF, HALF)

    def side(place, part):
        return jnp.dot(part, left_ref[at(place * HALF, HALF), cols].astype(F32), precision=HIGHEST, preferred_element_type=F32)

    for place, mine, beside in ((core, mine_ref, beside_ref), (1 - core, mine_other, beside_other)):
        left_done[at(place * width, width), :] = side(x_low, mine[...]) + side(1 - x_low, beside[...])
    for block in range(5):
        root = right_ref[block] if block < 4 else last_ref[...]
        span = slice(block * BS, (block + 1) * BS)
        done[:, span] = lax.dot_general(
            left_done[span, :], root.astype(F32), (((0,), (0,)), ((), ())), precision=HIGHEST, preferred_element_type=F32
        )
    out_ref[...] = (done[at(core * 64, 64, 64), :] * (1.0 / math.sqrt(TOKENS))).astype(BF16)


def apply_roots(where, pieces, left, right, last):
    width = 2 * pieces[0].shape[0]
    shape = jax.ShapeDtypeStruct((64, width), BF16)
    return call(
        apply_kernel,
        (1,),
        where,
        [whole(p) for p in (*pieces, left, right, last)],
        whole(shape),
        shape,
        (*pieces, left, right, last),
        scratch=[pltpu.VMEM((width, HALF), F32), pltpu.VMEM((HALF, width), F32)],
        limit=32,
    )


def swap(value, axis):
    return lax.ppermute(value, axis, [(0, 1), (1, 0)])


def away(value, axis, shift):
    if shift == 0:
        return value
    return lax.ppermute(value, axis, [(i, (i + shift) % 4) for i in range(4)])


def per_device(acts, grads, owners):
    zh, y, x, core, column = (lax.axis_index(a) for a in ("zh", "y", "x", "c", "mp"))
    x_high, x_low = x // 2, x % 2
    rows, width = grads.shape
    where = jnp.stack([column, core, x_low, x, y, zh]).astype(jnp.int32)

    with jax.named_scope("exchange"):
        acts_other = swap(acts, "c")
        grads_other = swap(grads, "c")

    with jax.named_scope("factors"):
        mine, sent = factor_parts(where, acts, grads)
        mine = mine + swap(sent, "c")
        mine = lax.all_to_all(mine.reshape(16 * 96, BS), ("y", "x"), 0, 0, tiled=True)

    with jax.named_scope("product"):
        inputs = (acts, acts_other, grads, grads_other)
        far = far_products(where, *inputs, where)
        near = list(near_products(where, *inputs, far[0]))
        came = [away(far[0], "x", 1), away(far[1], "x", 3), away(far[2], "y", 1), away(far[3], "y", 3)]
        home = list(home_products(where, *inputs, near[0]))
        mine, *came, home[0] = lax.optimization_barrier((mine, *came, home[0]))

    with jax.named_scope("sum_factors"):
        mine = fold(where, mine)
        near = merge(where, near, came, mine)
        mine = mine + swap(mine, "zh")
        mine = jnp.concatenate([mine, swap(mine[64:], "c")], axis=0)
        pieces = [away(mine, "y", shift) for shift in range(4)]

    with jax.named_scope("roots"):
        pieces[1], pieces[2], pieces[3], *near = lax.optimization_barrier((pieces[1], pieces[2], pieces[3], *near))
        passed = [away(near[0], "x", 1), away(near[1], "x", 3), away(near[2], "y", 1), away(near[3], "y", 3)]
        roots = two_roots(where, pieces, near[0])
        last_root = roots[1]
        four = jnp.broadcast_to(roots[0], (4, BS, BS)).reshape(4 * BS, BS)
        four = lax.all_to_all(four, "x", 0, 0, tiled=True)

    with jax.named_scope("route"):
        low, high = route(where, (home[0], *passed[:2]), (home[1], *passed[2:]), roots)
        four, low = lax.optimization_barrier((four, low))
        low = lax.all_to_all(low, "y", 0, 0, tiled=True)
        routed = [lax.dynamic_index_in_dim(high, lax.rem(x + shift, 4), 0, keepdims=False) for shift in SHIFTS]
        high = [away(v, "x", shift) for v, shift in zip(routed, SHIFTS, strict=True)]

    with jax.named_scope("share"):
        four = four.reshape(4, BS, BS)
        other_four = swap(four, "c")
        input_roots = jnp.where(core == 0, four, other_four)
        output_roots = jnp.where(core == 0, other_four, four)

    with jax.named_scope("left_root"):
        holder = zh * 2 + y // 2
        left = lax.dynamic_index_in_dim(input_roots, (y % 2) * 2 + x_high, 0, keepdims=False)
        got = jnp.zeros_like(left)
        for shift in range(1, 4):
            pairs = []
            for a in range(2):
                for b in range(4):
                    source = a * 2 + b // 2
                    pairs.append(((a * 4 + b) * 4 + source, (a * 4 + b) * 4 + (source + shift) % 4))
            got = got + lax.ppermute(left, ("zh", "y", "mp"), pairs)
        left = jnp.where(column == holder, left, got)

    with jax.named_scope("kept"):
        data_rank = ((zh * 4 + y) * 4 + x) * 2 + core
        owned = (owners[0] == data_rank).astype(jnp.int32)
        order = jnp.cumsum(owned) - 1
        slots = jnp.arange(MOST, dtype=jnp.int32)
        select = owned[None, :] * (order[None, :] == slots[:, None]).astype(jnp.int32)
        filled = jnp.sum(select, axis=1)
        place = jnp.argmax(select, axis=1)
        every = jnp.concatenate([input_roots, output_roots, last_root[None]], axis=0)
        kept = jnp.stack(
            [
                jnp.where(filled[s] > 0, lax.dynamic_index_in_dim(every, place[s], 0, keepdims=False), 0).astype(BF16)
                for s in range(MOST)
            ]
        )

    with jax.named_scope("finish"):
        stay, leave = settle(where, low, high, other_four)
        total = stay + swap(leave, "zh")
        total, left = lax.optimization_barrier((total, left))
        beside = lax.ppermute(total, "x", [(0, 1), (1, 0), (2, 3), (3, 2)])
        pieces = (total, beside, swap(total, "c"), swap(beside, "c"))
        update = apply_roots(where, pieces, left, output_roots, last_root)
    return update, kept


def solution(mesh):
    fine = Mesh(mesh.devices.reshape(2, 4, 4, 2, 4), ("zh", "y", "x", "c", "mp"))
    return jax.shard_map(
        per_device,
        mesh=fine,
        in_specs=(P(DP, None), P(DP, "mp"), P("mp", None)),
        out_specs=(P(DP, "mp"), P(DP, "mp", None)),
        check_vma=False,
    )
```

```python
import functools
import math

import jax
import jax.numpy as jnp
from jax import lax
from jax.experimental import pallas as pl
from jax.experimental.pallas import tpu as pltpu
from jax.sharding import Mesh, PartitionSpec as P

BS = 256
HALF = 128
ITERS = 12
MOST = 2
DAMPING = 0.1
TOKENS = 32768
DP = ("zh", "y", "x", "c")
HIGHEST = lax.Precision.HIGHEST
F32 = jnp.float32
BF16 = jnp.bfloat16


def tdot(lhs, rhs):
    return lax.dot_general(lhs, rhs, (((0,), (0,)), ((), ())), preferred_element_type=F32)


SMEM = pl.BlockSpec(memory_space=pltpu.SMEM)
ANY = pl.BlockSpec(memory_space=pl.ANY)
SHIFTS = (2, 1, 3, 0)


def at(start, size, step=HALF):
    return pl.ds(pl.multiple_of(start, step), size)


def whole(array):
    return pl.BlockSpec(array.shape, lambda *_: (0,) * len(array.shape))


def call(kernel, grid, scalars, in_specs, out_specs, out_shape, operands, scratch=(), limit=60, flops=0):
    return pl.pallas_call(
        kernel,
        grid_spec=pltpu.PrefetchScalarGridSpec(
            num_scalar_prefetch=1, grid=grid, in_specs=in_specs, out_specs=out_specs, scratch_shapes=scratch
        ),
        out_shape=out_shape,
        compiler_params=pltpu.CompilerParams(vmem_limit_bytes=limit * 2**20),
        cost_estimate=pl.CostEstimate(flops=flops, bytes_accessed=2**18, transcendentals=0),
    )(scalars, *operands)


def factor_kernel(where_ref, acts_ref, grads_ref, kept_ref, sent_ref):
    def write(out_ref, ref, half):
        for block in range(4):
            span = ref[:, block * BS : (block + 1) * BS]
            value = tdot(span, span)
            for row in range(4):
                first, last = slice(row * 32, row * 32 + 32), slice(HALF + row * 32, HALF + row * 32 + 32)
                out_ref[row, block, 0:32, :] = value[first, :HALF]
                out_ref[row, block, 32:64, :] = value[first, HALF:]
                out_ref[row, block, 64:96, :] = value[last, HALF:]
        span = grads_ref[:, 4 * BS :]
        value = tdot(span, span)
        for row in range(4):
            tile = value[half * HALF + row * 32 : half * HALF + row * 32 + 32, half * HALF : (half + 1) * HALF]
            corner = value[half * 64 + row * 16 : half * 64 + row * 16 + 16, HALF:]
            for block in range(4):
                out_ref[row, block, 96:128, :] = tile
                out_ref[row, block, 128:144, :] = corner

    @pl.when(where_ref[1] == 0)
    def _():
        write(kept_ref, acts_ref, 0)
        write(sent_ref, grads_ref, 1)

    @pl.when(where_ref[1] == 1)
    def _():
        write(sent_ref, acts_ref, 0)
        write(kept_ref, grads_ref, 1)


def factor_parts(where, acts, grads):
    rows = acts.shape[0]
    shape = jax.ShapeDtypeStruct((4, 4, 144, HALF), F32)
    return call(
        factor_kernel,
        (1,),
        where,
        [pl.BlockSpec((rows, 4 * BS), lambda i, w: (0, w[0])), whole(grads)],
        [whole(shape)] * 2,
        [shape] * 2,
        (acts, grads),
    )


def multiply_all(mine, other, grads_ref, grads_other):
    def multiply(left, right):
        return tdot(grads_ref[...], left) + tdot(grads_other[...], right)

    return (
        multiply(jnp.concatenate([r[...] for r in mine[:4]], axis=1), jnp.concatenate([r[...] for r in other[:4]], axis=1)),
        multiply(mine[4][...], other[4][...]),
    )


def far_kernel(where_ref, *refs):
    for part, value in enumerate(multiply_all(refs[0:5], refs[5:10], refs[10], refs[11])):
        for j in range(4):
            refs[13 + part * 2 + j // 2][j % 2] = value[:, j * HALF : (j + 1) * HALF]


def near_kernel(where_ref, *refs):
    outs, slots, sems = refs[13:17], refs[17], refs[18]
    step = pl.program_id(0)

    def copies(k):
        return [pltpu.make_async_copy(slots.at[k, part], outs[part * 2 + k], sems.at[k, part]) for part in range(2)]

    for k in range(2):

        @pl.when(step == k)
        def _(k=k):
            for part, value in enumerate(multiply_all(refs[0:5], refs[5:10], refs[10], refs[11])):
                for j in range(4):
                    slots[k, part, j] = value[:, j * HALF : (j + 1) * HALF]
            for copy in copies(k):
                copy.start()

    @pl.when(step == 1)
    def _():
        for k in range(2):
            for copy in copies(k):
                copy.wait()


def home_kernel(where_ref, *refs):
    for value, out in zip(multiply_all(refs[0:5], refs[5:10], refs[10], refs[11]), refs[13:15], strict=True):
        for j in range(4):
            out[j] = value[:, j * HALF : (j + 1) * HALF]


def product(kernel, where, shifts, acts, acts_other, grads, grads_other, earlier, out_specs, out_shape, **more):
    rows, width = grads.shape[0], grads.shape[1] // 2

    def there(place, i):
        shift = shifts[0]
        for k in range(1, len(shifts)):
            shift = jnp.where(i == k, shifts[k], shift)
        return lax.rem(place + shift, 4)

    lefts = [
        pl.BlockSpec((rows, HALF), functools.partial(lambda j, i, w: (0, 4 * j + there(w[3], i)), j)) for j in range(4)
    ] + [pl.BlockSpec((rows, 4 * HALF), lambda i, w: (0, 4 + there(w[4], i)))]
    columns = pl.BlockSpec((rows, width), lambda i, w: (0, w[1]))
    return call(
        kernel,
        (len(shifts),),
        where,
        lefts + lefts + [columns, columns, ANY],
        out_specs,
        out_shape,
        [acts] * 5 + [acts_other] * 5 + [grads, grads_other, earlier],
        **more,
    )


def far_products(where, *inputs):
    two = jax.ShapeDtypeStruct((2, inputs[2].shape[1] // 2, HALF), F32)
    return product(far_kernel, where, (2,), *inputs, [whole(two)] * 4, [two] * 4)


def near_products(where, *inputs):
    width = inputs[2].shape[1] // 2
    four = jax.ShapeDtypeStruct((4, width, HALF), F32)
    scratch = [pltpu.VMEM((2, 2, 4, width, HALF), F32), pltpu.SemaphoreType.DMA((2, 2))]
    return product(near_kernel, where, (1, 3), *inputs, [ANY] * 4, [four] * 4, scratch=scratch)


def home_products(where, *inputs):
    four = jax.ShapeDtypeStruct((4, inputs[2].shape[1] // 2, HALF), F32)
    return product(home_kernel, where, (0,), *inputs, [whole(four)] * 2, [four] * 2)


def merge_kernel(_, *refs):
    for k in range(4):
        refs[9 + k][...] = refs[k][...] + refs[4 + k][...]


def merge(where, near, came, earlier):
    shape = near[0].shape
    block = (1, *shape[1:])
    low = pl.BlockSpec(block, lambda i, w: (i, 0, 0))
    high = pl.BlockSpec(block, lambda i, w: (2 + i, 0, 0))
    return pl.pallas_call(
        merge_kernel,
        grid_spec=pltpu.PrefetchScalarGridSpec(
            num_scalar_prefetch=1,
            grid=(2,),
            in_specs=[low, high, low, high] + [low] * 4 + [ANY],
            out_specs=[low, high, low, high],
        ),
        out_shape=[jax.ShapeDtypeStruct(shape, F32)] * 4,
        input_output_aliases={1: 0, 2: 1, 3: 2, 4: 3},
        compiler_params=pltpu.CompilerParams(vmem_limit_bytes=60 * 2**20),
        cost_estimate=pl.CostEstimate(flops=0, bytes_accessed=2**18, transcendentals=0),
    )(where, *near, *came, earlier)


def route_kernel(where_ref, *refs):
    step = pl.program_id(0)
    outs = refs[7:]
    for part in range(2):
        own, below, above = refs[part * 3 : part * 3 + 3]
        distance = lax.rem(step + 4 - where_ref[4 - part], 4)
        value = own[0] + (below[0] + above[0])
        for k, shift in enumerate(SHIFTS):
            for keep in range(2):

                @pl.when(jnp.logical_and(distance == shift, (where_ref[5] == part) == (keep == 1)))
                def _(out=outs[keep * 4 + k], value=value):
                    out[...] = value


def route(where, first, second, earlier):
    shape = jax.ShapeDtypeStruct(first[0].shape[1:], F32)
    every = pl.BlockSpec((1, *shape.shape), lambda i, w: (i, 0, 0))
    outs = call(
        route_kernel,
        (4,),
        where,
        [every] * 6 + [ANY],
        [whole(shape)] * 8,
        [shape] * 8,
        (*first, *second, earlier),
    )
    return list(outs[:4]), list(outs[4:])


def sum_kernel(_, *refs):
    refs[5][...] = (refs[3][...] + refs[0][...]) + (refs[1][...] + refs[2][...])


def sum_four(where, parts, earlier):
    shape = jax.ShapeDtypeStruct(parts[0].shape, F32)
    return call(sum_kernel, (1,), where, [whole(shape)] * 4 + [ANY], whole(shape), shape, (*parts, earlier))


def along(value, shift, keep):
    if shift == 0:
        return value
    pairs = []
    for z in range(2):
        for i in range(4):
            for j in range(4):
                y, x = ((i + shift) % 4, j) if (z == 0) == keep else (i, (j + shift) % 4)
                pairs.append(((z * 4 + i) * 4 + j, (z * 4 + y) * 4 + x))
    return lax.ppermute(value, ("zh", "y", "x"), pairs)


def fold_kernel(_, in_ref, out_ref):
    rows = out_ref.shape[0]
    total = in_ref[0:rows]
    for source in range(1, 16):
        total = total + in_ref[source * rows : (source + 1) * rows]
    out_ref[...] = total


def fold(where, parts):
    shape = jax.ShapeDtypeStruct((parts.shape[0] // 16, parts.shape[1]), F32)
    return call(fold_kernel, (1,), where, [whole(parts)], whole(shape), shape, (parts,), limit=16)


def root_kernel(where_ref, p0, p1, p2, p3, _, out_ref, block_ref, last):
    core = where_ref[1]
    for shift, piece in enumerate((p0, p1, p2, p3)):
        place = lax.rem(where_ref[4] + 4 - shift, 4)
        first, second = at(place * 32, 32, 32), at(HALF + place * 32, 32, 32)
        block_ref[first, :HALF] = piece[0:32]
        block_ref[first, HALF:] = piece[32:64]
        block_ref[second, HALF:] = piece[64:96]
        for half, wanted in ((0, core == 0), (1, core == 1)):

            @pl.when(wanted)
            def _(half=half, piece=piece, place=place, first=first, second=second):
                start = 96 if half == 0 else 144
                last[first, :HALF] = piece[start : start + 32]
                last[at(place * 16, 16, 16), HALF:] = piece[start + 32 : start + 48]
                start = 240 - start
                last[second, HALF:] = piece[start : start + 32]
                last[at(64 + place * 16, 16, 16), HALF:] = piece[start + 32 : start + 48]

    block_ref[HALF:, :HALF] = block_ref[:HALF, HALF:].T
    last[HALF:, :HALF] = last[:HALF, HALF:].T
    row = lax.broadcasted_iota(jnp.int32, (BS, BS), 0)
    col = lax.broadcasted_iota(jnp.int32, (BS, BS), 1)
    identity = jnp.where(row == col, 1.0, 0.0).astype(F32)
    mul = functools.partial(jnp.dot, precision=HIGHEST, preferred_element_type=F32)

    def start(summed):
        factor = summed * (1.0 / TOKENS) + DAMPING * identity
        norm = jnp.sqrt(jnp.sum(factor * factor, keepdims=True))
        current = factor / norm
        step = 1.5 * identity - 0.5 * current
        return norm, mul(current, step), step

    norm_a, cur_a, est_a = start(block_ref[...])
    norm_b, cur_b, est_b = start(last[...])

    def advance(_, carry):
        cur_a, est_a, cur_b, est_b = carry
        step_a = 1.5 * identity - 0.5 * mul(est_a, cur_a)
        step_b = 1.5 * identity - 0.5 * mul(est_b, cur_b)
        return mul(cur_a, step_a), mul(step_a, est_a), mul(cur_b, step_b), mul(step_b, est_b)

    cur_a, est_a, cur_b, est_b = lax.fori_loop(0, ITERS - 2, advance, (cur_a, est_a, cur_b, est_b))
    step_a = 1.5 * identity - 0.5 * mul(est_a, cur_a)
    step_b = 1.5 * identity - 0.5 * mul(est_b, cur_b)
    out_ref[0] = (mul(step_a, est_a) / jnp.sqrt(norm_a)).astype(BF16)
    out_ref[1] = (mul(step_b, est_b) / jnp.sqrt(norm_b)).astype(BF16)


def two_roots(where, pieces, earlier):
    shape = jax.ShapeDtypeStruct((2, BS, BS), BF16)
    return call(
        root_kernel,
        (1,),
        where,
        [whole(p) for p in pieces] + [ANY],
        whole(shape),
        shape,
        (*pieces, earlier),
        scratch=[pltpu.VMEM((BS, BS), F32), pltpu.VMEM((BS, BS), F32)],
        limit=32,
    )


def apply_kernel(
    where_ref, mine_ref, beside_ref, mine_other, beside_other, left_ref, input_ref, right_ref, last_ref, out_ref, kept_ref, left_done, done
):
    core, x_low = where_ref[1], where_ref[2]
    width = mine_ref.shape[0]
    cols = at(x_low * HALF, HALF)

    def side(place, part):
        return jnp.dot(part, left_ref[at(place * HALF, HALF), cols].astype(F32), precision=HIGHEST, preferred_element_type=F32)

    for place, mine, beside in ((core, mine_ref, beside_ref), (1 - core, mine_other, beside_other)):
        left_done[at(place * width, width), :] = side(x_low, mine[...]) + side(1 - x_low, beside[...])
    for block in range(5):
        root = right_ref[block] if block < 4 else last_ref[...]
        span = slice(block * BS, (block + 1) * BS)
        done[:, span] = lax.dot_general(
            left_done[span, :], root.astype(F32), (((0,), (0,)), ((), ())), precision=HIGHEST, preferred_element_type=F32
        )
    out_ref[...] = (done[at(core * 64, 64, 64), :] * (1.0 / math.sqrt(TOKENS))).astype(BF16)
    kept_ref[...] = jnp.zeros_like(kept_ref)
    count = jnp.int32(0)
    for block in range(9):
        root = input_ref.at[block] if block < 4 else right_ref.at[block - 4] if block < 8 else last_ref
        owned = where_ref[7 + block] == where_ref[6]
        for slot in range(MOST):

            @pl.when(jnp.logical_and(owned, count == slot))
            def _(root=root, slot=slot):
                kept_ref[slot] = root[...]

        count = count + owned.astype(jnp.int32)


def apply_roots(where, pieces, left, inputs, right, last):
    width = 2 * pieces[0].shape[0]
    shape = jax.ShapeDtypeStruct((64, width), BF16)
    kept = jax.ShapeDtypeStruct((MOST, BS, BS), BF16)
    return call(
        apply_kernel,
        (1,),
        where,
        [whole(p) for p in (*pieces, left, inputs, right, last)],
        [whole(shape), whole(kept)],
        [shape, kept],
        (*pieces, left, inputs, right, last),
        scratch=[pltpu.VMEM((width, HALF), F32), pltpu.VMEM((HALF, width), F32)],
        limit=32,
    )


def swap(value, axis):
    return lax.ppermute(value, axis, [(0, 1), (1, 0)])


def away(value, axis, shift):
    if shift == 0:
        return value
    return lax.ppermute(value, axis, [(i, (i + shift) % 4) for i in range(4)])


def per_device(acts, grads, owners):
    zh, y, x, core, column = (lax.axis_index(a) for a in ("zh", "y", "x", "c", "mp"))
    x_high, x_low = x // 2, x % 2
    rows, width = grads.shape
    data_rank = ((zh * 4 + y) * 4 + x) * 2 + core
    places = jnp.stack([column, core, x_low, x, y, zh, data_rank]).astype(jnp.int32)
    where = places[:6]

    with jax.named_scope("factors"):
        mine, sent = factor_parts(where, acts, grads)
        sent = swap(sent, "c")
        sent, acts_late, grads_late = lax.optimization_barrier((sent, acts, grads))
        mine = mine + sent
        mine = lax.all_to_all(mine.reshape(16 * 144, HALF), ("y", "x"), 0, 0, tiled=True)

    with jax.named_scope("exchange"):
        acts_other = swap(acts_late, "c")
        grads_other = swap(grads_late, "c")

    with jax.named_scope("product"):
        inputs = (acts, acts_other, grads, grads_other)
        far = far_products(where, *inputs, where)
        near = list(near_products(where, *inputs, far[0]))
        came = [away(far[0], "x", 1), away(far[1], "x", 3), away(far[2], "y", 1), away(far[3], "y", 3)]
        mine, near[0] = lax.optimization_barrier((mine, near[0]))

    with jax.named_scope("sum_factors"):
        mine = fold(where, mine)
        home = home_products(where, *inputs, mine)
        near = list(merge(where, near, came, home[0]))
        mine, near[0] = lax.optimization_barrier((mine + swap(mine, "zh"), near[0]))
        mine = jnp.concatenate([mine, swap(mine[96:], "c")], axis=0)
        pieces = [away(mine, "y", shift) for shift in range(4)]

    with jax.named_scope("roots"):
        pieces[1], pieces[2], pieces[3], near[2], near[3] = lax.optimization_barrier((*pieces[1:], near[2], near[3]))
        passed = [away(near[0], "x", 1), away(near[1], "x", 3), away(near[2], "y", 1), away(near[3], "y", 3)]
        roots = two_roots(where, pieces, near[0])
        last_root = roots[1]
        four = jnp.broadcast_to(roots[0], (4, BS, BS)).reshape(4 * BS, BS)
        four = lax.all_to_all(four, "x", 0, 0, tiled=True)

    with jax.named_scope("route"):
        other, own = route(where, (home[0], *passed[:2]), (home[1], *passed[2:]), roots)
        far_plane = [along(v, shift, False) for v, shift in zip(other, SHIFTS, strict=True)]
        this_plane = [along(v, shift, True) for v, shift in zip(own, SHIFTS, strict=True)]
        four, own[3] = lax.optimization_barrier((four, own[3]))
        leave = sum_four(where, far_plane, four)
        four, leave = lax.optimization_barrier((four, leave))

    with jax.named_scope("share"):
        four = four.reshape(4, BS, BS)
        other_four = swap(four, "c")
        input_roots = jnp.where(core == 0, four, other_four)
        output_roots = jnp.where(core == 0, other_four, four)

    with jax.named_scope("finish"):
        came_over = swap(leave, "zh")

    with jax.named_scope("left_root"):
        holder = zh * 2 + y // 2
        left = lax.dynamic_index_in_dim(input_roots, (y % 2) * 2 + x_high, 0, keepdims=False)
        left, this_plane[0] = lax.optimization_barrier((left, this_plane[0]))
        got = jnp.zeros_like(left)
        for shift in range(1, 4):
            pairs = []
            for a in range(2):
                for b in range(4):
                    source = a * 2 + b // 2
                    pairs.append(((a * 4 + b) * 4 + source, (a * 4 + b) * 4 + (source + shift) % 4))
            got = got + lax.ppermute(left, ("zh", "y", "mp"), pairs)
        left = jnp.where(column == holder, left, got)

    with jax.named_scope("finish"):
        total = sum_four(where, [*this_plane[:3], own[3]], leave) + came_over
        beside = lax.ppermute(total, "x", [(0, 1), (1, 0), (2, 3), (3, 2)])
        pieces = (total, beside, swap(total, "c"), swap(beside, "c"))
        update, kept = apply_roots(jnp.concatenate([places, owners[0]]), pieces, left, input_roots, output_roots, last_root)
    return update, kept


def solution(mesh):
    fine = Mesh(mesh.devices.reshape(2, 4, 4, 2, 4), ("zh", "y", "x", "c", "mp"))
    return jax.shard_map(
        per_device,
        mesh=fine,
        in_specs=(P(DP, None), P(DP, "mp"), P("mp", None)),
        out_specs=(P(DP, "mp"), P(DP, "mp", None)),
        check_vma=False,
    )
```

```python
import functools
import math

import jax
import jax.numpy as jnp
from jax import lax
from jax.experimental import pallas as pl
from jax.experimental.pallas import tpu as pltpu
from jax.sharding import Mesh, PartitionSpec as P

BS = 256
HALF = 128
ITERS = 12
MOST = 2
DAMPING = 0.1
TOKENS = 32768
DP = ("zh", "y", "x", "c")
HIGHEST = lax.Precision.HIGHEST
F32 = jnp.float32
BF16 = jnp.bfloat16


def tdot(lhs, rhs):
    return lax.dot_general(lhs, rhs, (((0,), (0,)), ((), ())), preferred_element_type=F32)


SMEM = pl.BlockSpec(memory_space=pltpu.SMEM)
ANY = pl.BlockSpec(memory_space=pl.ANY)
SHIFTS = (2, 1, 3, 0)


def at(start, size, step=HALF):
    return pl.ds(pl.multiple_of(start, step), size)


def whole(array):
    return pl.BlockSpec(array.shape, lambda *_: (0,) * len(array.shape))


def call(kernel, grid, scalars, in_specs, out_specs, out_shape, operands, scratch=(), limit=60, flops=0):
    return pl.pallas_call(
        kernel,
        grid_spec=pltpu.PrefetchScalarGridSpec(
            num_scalar_prefetch=1, grid=grid, in_specs=in_specs, out_specs=out_specs, scratch_shapes=scratch
        ),
        out_shape=out_shape,
        compiler_params=pltpu.CompilerParams(vmem_limit_bytes=limit * 2**20),
        cost_estimate=pl.CostEstimate(flops=flops, bytes_accessed=2**18, transcendentals=0),
    )(scalars, *operands)


def factor_kernel(where_ref, acts_ref, grads_ref, kept_ref, sent_ref):
    def write(out_ref, ref, half):
        for block in range(4):
            span = ref[:, block * BS : (block + 1) * BS]
            value = tdot(span, span)
            for row in range(4):
                first, last = slice(row * 32, row * 32 + 32), slice(HALF + row * 32, HALF + row * 32 + 32)
                out_ref[row, block, 0:32, :] = value[first, :HALF]
                out_ref[row, block, 32:64, :] = value[first, HALF:]
                out_ref[row, block, 64:96, :] = value[last, HALF:]
        span = grads_ref[:, 4 * BS :]
        value = tdot(span, span)
        for row in range(4):
            tile = value[half * HALF + row * 32 : half * HALF + row * 32 + 32, half * HALF : (half + 1) * HALF]
            corner = value[half * 64 + row * 16 : half * 64 + row * 16 + 16, HALF:]
            for block in range(4):
                out_ref[row, block, 96:128, :] = tile
                out_ref[row, block, 128:144, :] = corner

    @pl.when(where_ref[1] == 0)
    def _():
        write(kept_ref, acts_ref, 0)
        write(sent_ref, grads_ref, 1)

    @pl.when(where_ref[1] == 1)
    def _():
        write(sent_ref, acts_ref, 0)
        write(kept_ref, grads_ref, 1)


def factor_parts(where, acts, grads):
    rows = acts.shape[0]
    shape = jax.ShapeDtypeStruct((4, 4, 144, HALF), F32)
    return call(
        factor_kernel,
        (1,),
        where,
        [pl.BlockSpec((rows, 4 * BS), lambda i, w: (0, w[0])), whole(grads)],
        [whole(shape)] * 2,
        [shape] * 2,
        (acts, grads),
    )


def multiply_all(mine, other, grads_ref, grads_other):
    def multiply(left, right):
        return tdot(grads_ref[...], left) + tdot(grads_other[...], right)

    return (
        multiply(jnp.concatenate([r[...] for r in mine[:4]], axis=1), jnp.concatenate([r[...] for r in other[:4]], axis=1)),
        multiply(mine[4][...], other[4][...]),
    )


def far_kernel(where_ref, *refs):
    for part, value in enumerate(multiply_all(refs[0:5], refs[5:10], refs[10], refs[11])):
        for j in range(4):
            refs[13 + part * 2 + j // 2][j % 2] = value[:, j * HALF : (j + 1) * HALF]


def near_kernel(where_ref, *refs):
    outs, slots, sems = refs[13:17], refs[17], refs[18]
    step = pl.program_id(0)

    def copies(k):
        return [pltpu.make_async_copy(slots.at[k, part], outs[part * 2 + k], sems.at[k, part]) for part in range(2)]

    for k in range(2):

        @pl.when(step == k)
        def _(k=k):
            for part, value in enumerate(multiply_all(refs[0:5], refs[5:10], refs[10], refs[11])):
                for j in range(4):
                    slots[k, part, j] = value[:, j * HALF : (j + 1) * HALF]
            for copy in copies(k):
                copy.start()

    @pl.when(step == 1)
    def _():
        for k in range(2):
            for copy in copies(k):
                copy.wait()


def home_kernel(where_ref, *refs):
    for value, out in zip(multiply_all(refs[0:5], refs[5:10], refs[10], refs[11]), refs[13:15], strict=True):
        for j in range(4):
            out[j] = value[:, j * HALF : (j + 1) * HALF]


def product(kernel, where, shifts, acts, acts_other, grads, grads_other, earlier, out_specs, out_shape, **more):
    rows, width = grads.shape[0], grads.shape[1] // 2

    def there(place, i):
        shift = shifts[0]
        for k in range(1, len(shifts)):
            shift = jnp.where(i == k, shifts[k], shift)
        return lax.rem(place + shift, 4)

    lefts = [
        pl.BlockSpec((rows, HALF), functools.partial(lambda j, i, w: (0, 4 * j + there(w[3], i)), j)) for j in range(4)
    ] + [pl.BlockSpec((rows, 4 * HALF), lambda i, w: (0, 4 + there(w[4], i)))]
    columns = pl.BlockSpec((rows, width), lambda i, w: (0, w[1]))
    return call(
        kernel,
        (len(shifts),),
        where,
        lefts + lefts + [columns, columns, ANY],
        out_specs,
        out_shape,
        [acts] * 5 + [acts_other] * 5 + [grads, grads_other, earlier],
        **more,
    )


def far_products(where, *inputs):
    two = jax.ShapeDtypeStruct((2, inputs[2].shape[1] // 2, HALF), F32)
    return product(far_kernel, where, (2,), *inputs, [whole(two)] * 4, [two] * 4)


def near_products(where, *inputs):
    width = inputs[2].shape[1] // 2
    four = jax.ShapeDtypeStruct((4, width, HALF), F32)
    scratch = [pltpu.VMEM((2, 2, 4, width, HALF), F32), pltpu.SemaphoreType.DMA((2, 2))]
    return product(near_kernel, where, (1, 3), *inputs, [ANY] * 4, [four] * 4, scratch=scratch)


def home_products(where, *inputs):
    four = jax.ShapeDtypeStruct((4, inputs[2].shape[1] // 2, HALF), F32)
    return product(home_kernel, where, (0,), *inputs, [whole(four)] * 2, [four] * 2)


def merge_kernel(_, *refs):
    for k in range(4):
        refs[9 + k][...] = refs[k][...] + refs[4 + k][...]


def merge(where, near, came, earlier):
    shape = near[0].shape
    block = (1, *shape[1:])
    low = pl.BlockSpec(block, lambda i, w: (i, 0, 0))
    high = pl.BlockSpec(block, lambda i, w: (2 + i, 0, 0))
    return pl.pallas_call(
        merge_kernel,
        grid_spec=pltpu.PrefetchScalarGridSpec(
            num_scalar_prefetch=1,
            grid=(2,),
            in_specs=[low, high, low, high] + [low] * 4 + [ANY],
            out_specs=[low, high, low, high],
        ),
        out_shape=[jax.ShapeDtypeStruct(shape, F32)] * 4,
        input_output_aliases={1: 0, 2: 1, 3: 2, 4: 3},
        compiler_params=pltpu.CompilerParams(vmem_limit_bytes=60 * 2**20),
        cost_estimate=pl.CostEstimate(flops=0, bytes_accessed=2**18, transcendentals=0),
    )(where, *near, *came, earlier)


def route_kernel(where_ref, *refs):
    step = pl.program_id(0)
    outs = refs[7:]
    for part in range(2):
        own, below, above = refs[part * 3 : part * 3 + 3]
        distance = lax.rem(step + 4 - where_ref[4 - part], 4)
        value = own[0] + (below[0] + above[0])
        for k, shift in enumerate(SHIFTS):
            for keep in range(2):

                @pl.when(jnp.logical_and(distance == shift, (where_ref[5] == part) == (keep == 1)))
                def _(out=outs[keep * 4 + k], value=value):
                    out[...] = value


def route(where, first, second, earlier):
    shape = jax.ShapeDtypeStruct(first[0].shape[1:], F32)
    every = pl.BlockSpec((1, *shape.shape), lambda i, w: (i, 0, 0))
    outs = call(
        route_kernel,
        (4,),
        where,
        [every] * 6 + [ANY],
        [whole(shape)] * 8,
        [shape] * 8,
        (*first, *second, earlier),
    )
    return list(outs[:4]), list(outs[4:])


def along(value, shift, keep):
    if shift == 0:
        return value
    pairs = []
    for z in range(2):
        for i in range(4):
            for j in range(4):
                y, x = ((i + shift) % 4, j) if (z == 0) == keep else (i, (j + shift) % 4)
                pairs.append(((z * 4 + i) * 4 + j, (z * 4 + y) * 4 + x))
    return lax.ppermute(value, ("zh", "y", "x"), pairs)


def fold_kernel(_, in_ref, out_ref):
    rows = out_ref.shape[0]
    total = in_ref[0:rows]
    for source in range(1, 16):
        total = total + in_ref[source * rows : (source + 1) * rows]
    out_ref[...] = total


def fold(where, parts):
    shape = jax.ShapeDtypeStruct((parts.shape[0] // 16, parts.shape[1]), F32)
    return call(fold_kernel, (1,), where, [whole(parts)], whole(shape), shape, (parts,), limit=16)


def root_kernel(where_ref, p0, p1, p2, p3, mine_ref, other_ref, _, out_ref, summed_ref, root_ref):
    core, x, y = where_ref[1], where_ref[3], where_ref[4]
    for shift, piece in enumerate((p0, p1, p2, p3)):
        place = lax.rem(y + 4 - shift, 4)
        first, second = at(place * 32, 32, 32), at(HALF + place * 32, 32, 32)

        @pl.when(y < 3)
        def _(piece=piece, first=first, second=second):
            summed_ref[first, :HALF] = piece[0:32]
            summed_ref[first, HALF:] = piece[32:64]
            summed_ref[second, HALF:] = piece[64:96]

        for half in range(2):

            @pl.when(jnp.logical_and(y == 3, core == half))
            def _(half=half, shift=shift, place=place, first=first, second=second):
                upper, lower = (mine_ref, other_ref) if half == 0 else (other_ref, mine_ref)
                tile, corner = slice(shift * 48, shift * 48 + 32), slice(shift * 48 + 32, shift * 48 + 48)
                summed_ref[first, :HALF] = upper[tile]
                summed_ref[at(place * 16, 16, 16), HALF:] = upper[corner]
                summed_ref[second, HALF:] = lower[tile]
                summed_ref[at(64 + place * 16, 16, 16), HALF:] = lower[corner]

    summed_ref[HALF:, :HALF] = summed_ref[:HALF, HALF:].T
    row = lax.broadcasted_iota(jnp.int32, (BS, BS), 0)
    col = lax.broadcasted_iota(jnp.int32, (BS, BS), 1)
    identity = jnp.where(row == col, 1.0, 0.0).astype(F32)
    mul = functools.partial(jnp.dot, precision=HIGHEST, preferred_element_type=F32)
    factor = summed_ref[...] * (1.0 / TOKENS) + DAMPING * identity
    norm = jnp.sqrt(jnp.sum(factor * factor, keepdims=True))
    current = factor / norm
    step = 1.5 * identity - 0.5 * current

    def advance(_, carry):
        current, estimate = carry
        step = 1.5 * identity - 0.5 * mul(estimate, current)
        return mul(current, step), mul(step, estimate)

    current, estimate = lax.fori_loop(0, ITERS - 2, advance, (mul(current, step), step))
    step = 1.5 * identity - 0.5 * mul(estimate, current)
    root_ref[...] = (mul(step, estimate) / jnp.sqrt(norm)).astype(BF16)
    slab = root_ref[at(jnp.minimum(jnp.where(y < 3, 96 * y, 64 * x), 160), 96, 32), :]
    for place in range(16):
        out_ref[place] = slab


def root_slabs(where, pieces, earlier):
    shape = jax.ShapeDtypeStruct((16, 96, BS), BF16)
    return call(
        root_kernel,
        (1,),
        where,
        [whole(p) for p in pieces] + [ANY],
        whole(shape),
        shape,
        (*pieces, earlier),
        scratch=[pltpu.VMEM((BS, BS), F32), pltpu.VMEM((BS, BS), BF16)],
        limit=32,
    )


def thrice(value, root, contract):
    high = value.astype(BF16)
    rest = value - high.astype(F32)
    middle = rest.astype(BF16)
    low = (rest - middle.astype(F32)).astype(BF16)
    multiply = functools.partial(lax.dot_general, dimension_numbers=(contract, ((), ())), preferred_element_type=F32)
    return multiply(high, root) + (multiply(middle, root) + multiply(low, root))


def apply_kernel(
    where_ref, mine_ref, beside_ref, mine_other, beside_other, left_ref, input_ref, right_ref, last_ref, out_ref, kept_ref, left_done, done
):
    core, x_low = where_ref[1], where_ref[2]
    width = mine_ref.shape[0]
    cols = at(x_low * HALF, HALF)

    def side(place, part):
        return thrice(part, left_ref[0, at(place * HALF, HALF), cols], ((1,), (0,)))

    for place, mine, beside in ((core, mine_ref, beside_ref), (1 - core, mine_other, beside_other)):
        left_done[at(place * width, width), :] = side(x_low, mine[...]) + side(1 - x_low, beside[...])
    for block in range(5):
        root = right_ref[block] if block < 4 else last_ref[...]
        span = slice(block * BS, (block + 1) * BS)
        done[:, span] = thrice(left_done[span, :], root, ((0,), (0,)))
    out_ref[...] = (done[at(core * 64, 64, 64), :] * (1.0 / math.sqrt(TOKENS))).astype(BF16)
    kept_ref[...] = jnp.zeros_like(kept_ref)
    count = jnp.int32(0)
    for block in range(9):
        root = input_ref.at[block] if block < 4 else right_ref.at[block - 4] if block < 8 else last_ref
        owned = where_ref[7 + block] == where_ref[6]
        for slot in range(MOST):

            @pl.when(jnp.logical_and(owned, count == slot))
            def _(root=root, slot=slot):
                kept_ref[slot] = root[...]

        count = count + owned.astype(jnp.int32)


def apply_roots(where, pieces, left, inputs, right, last):
    width = 2 * pieces[0].shape[0]
    shape = jax.ShapeDtypeStruct((64, width), BF16)
    kept = jax.ShapeDtypeStruct((MOST, BS, BS), BF16)
    return call(
        apply_kernel,
        (1,),
        where,
        [whole(p) for p in pieces]
        + [pl.BlockSpec((1, BS, BS), lambda i, w: (w[5] * 2 + w[4] // 2, 0, 0))]
        + [whole(p) for p in (inputs, right, last)],
        [whole(shape), whole(kept)],
        [shape, kept],
        (*pieces, left, inputs, right, last),
        scratch=[pltpu.VMEM((width, HALF), F32), pltpu.VMEM((HALF, width), F32)],
        limit=32,
    )


def swap(value, axis):
    return lax.ppermute(value, axis, [(0, 1), (1, 0)])


def away(value, axis, shift):
    if shift == 0:
        return value
    return lax.ppermute(value, axis, [(i, (i + shift) % 4) for i in range(4)])


def per_device(acts, grads, owners):
    zh, y, x, core, column = (lax.axis_index(a) for a in ("zh", "y", "x", "c", "mp"))
    x_high, x_low = x // 2, x % 2
    rows, width = grads.shape
    data_rank = ((zh * 4 + y) * 4 + x) * 2 + core
    places = jnp.stack([column, core, x_low, x, y, zh, data_rank]).astype(jnp.int32)
    where = places[:6]

    with jax.named_scope("factors"):
        mine, sent = factor_parts(where, acts, grads)
        sent = swap(sent, "c")
        sent, acts_late, grads_late = lax.optimization_barrier((sent, acts, grads))
        mine = mine + sent
        mine = lax.all_to_all(mine.reshape(16 * 144, HALF), ("y", "x"), 0, 0, tiled=True)

    with jax.named_scope("exchange"):
        acts_other = swap(acts_late, "c")
        grads_other = swap(grads_late, "c")

    with jax.named_scope("product"):
        inputs = (acts, acts_other, grads, grads_other)
        far = far_products(where, *inputs, where)
        near = list(near_products(where, *inputs, far[0]))
        came = [away(far[0], "x", 1), away(far[1], "x", 3), away(far[2], "y", 1), away(far[3], "y", 3)]
        mine, near[0] = lax.optimization_barrier((mine, near[0]))

    with jax.named_scope("sum_factors"):
        mine = fold(where, mine)
        near = list(merge(where, near, came, mine))
        home = list(home_products(where, *inputs, near[0]))
        mine, near[0] = lax.optimization_barrier((mine + swap(mine, "zh"), near[0]))
        pieces = [away(mine, "y", shift) for shift in range(4)]

    with jax.named_scope("roots"):
        pieces[1], pieces[2], pieces[3], near[2], near[3] = lax.optimization_barrier((*pieces[1:], near[2], near[3]))
        passed = [away(near[0], "x", 1), away(near[1], "x", 3), away(near[2], "y", 1), away(near[3], "y", 3)]
        lasts = jnp.concatenate([v[96:] for v in pieces], axis=0)
        slabs = root_slabs(where, (*pieces, lasts, swap(lasts, "c")), near[0])
        slabs, home[0] = lax.optimization_barrier((slabs, home[0]))
        four = lax.all_to_all(slabs.reshape(16 * 96, BS), ("y", "x"), 0, 0, tiled=True)

    with jax.named_scope("route"):
        other, own = route(where, (home[0], *passed[:2]), (home[1], *passed[2:]), slabs)
        far_plane = [along(v, shift, False) for v, shift in zip(other, SHIFTS, strict=True)]
        this_plane = [along(v, shift, True) for v, shift in zip(own, SHIFTS, strict=True)]
        four, own[3] = lax.optimization_barrier((four, own[3]))
        far_plane[2], this_plane[1], this_plane[2] = lax.optimization_barrier((far_plane[2], this_plane[1], this_plane[2]))
        leave = (far_plane[3] + far_plane[0]) + (far_plane[1] + far_plane[2])
        four, leave = lax.optimization_barrier((four, leave))

    with jax.named_scope("share"):
        slabs = four.reshape(4, 4, 96, BS)
        four = jnp.concatenate([slabs[0], slabs[1], slabs[2, :, 32:]], axis=1)
        last_root = jnp.concatenate([slabs[3, 0, :64], slabs[3, 1, :64], slabs[3, 2, :64], slabs[3, 3, 32:]], axis=0)
        other_four = swap(four, "c")
        input_roots = jnp.where(core == 0, four, other_four)
        output_roots = jnp.where(core == 0, other_four, four)

    with jax.named_scope("finish"):
        came_over = swap(leave, "zh")

    with jax.named_scope("left_root"):
        left = lax.dynamic_index_in_dim(input_roots, (y % 2) * 2 + x_high, 0, keepdims=False)
        left, this_plane[0] = lax.optimization_barrier((left, this_plane[0]))
        left = jnp.broadcast_to(left, (4, BS, BS)).reshape(4 * BS, BS)
        left = lax.all_to_all(left, "mp", 0, 0, tiled=True).reshape(4, BS, BS)

    with jax.named_scope("finish"):
        total = ((own[3] + this_plane[0]) + (this_plane[1] + this_plane[2])) + came_over
        beside = lax.ppermute(total, "x", [(0, 1), (1, 0), (2, 3), (3, 2)])
        pieces = (total, beside, swap(total, "c"), swap(beside, "c"))
        update, kept = apply_roots(jnp.concatenate([places, owners[0]]), pieces, left, input_roots, output_roots, last_root)
    return update, kept


def solution(mesh):
    fine = Mesh(mesh.devices.reshape(2, 4, 4, 2, 4), ("zh", "y", "x", "c", "mp"))
    return jax.shard_map(
        per_device,
        mesh=fine,
        in_specs=(P(DP, None), P(DP, "mp"), P("mp", None)),
        out_specs=(P(DP, "mp"), P(DP, "mp", None)),
        check_vma=False,
    )
```
